32 devices in a mesh: grp: 4 (over y, x), col: 8 (over z, core).
Axes of the slice: x: 2, y: 2, z: 4, core: 2. Of those that a mesh axis runs over, the one named last changes fastest.
Arguments:
- blocks: bfloat16 [6144, 32, 1024], P(('grp', 'col'))
- i_index: int32 [6144], P(('grp', 'col')), may hold values from 0 to 15
- j_index: int32 [6144], P(('grp', 'col')), may hold values from 0 to 63
- k_index: int32 [6144], P(('grp', 'col')), may hold values from 0 to 15
- block_count: int32 [32], P(('grp', 'col')), may hold values from 24 to 192, as said below
- b_factor: float32 [16384, 256], P(('grp', 'col'))
- c_factor: float32 [4096, 256], P(('grp', 'col'))
Outputs:
- a_update: float32 [2048, 256], P(('grp', 'col'))
- b_update: float32 [16384, 256], P(('grp', 'col'))
The draws below stay inside these ranges and needn't reach their ends.
Inputs may be any that keep to these rules, and one draw needn't show every extreme that they name: block_count[d] is the number of live slots of device d = 8 * (grp index) + (col index): its slots d * 192 to d * 192 + block_count[d] - 1; every other slot is ignored. Some device has exactly 192 live slots.
All inputs are finite; a program needn't handle non-finite values.
Results may differ from the reference program's by a relative error of at most 0.005.
The reference program's roundings to bfloat16 on the way count: a program that leaves them out, or rounds other values in their place, can miss the bound.
Values may be sent and summed in bfloat16 or wider, within the bound.
A program may use at most 128 MiB of HBM per device.

```python
import math
import jax
import jax.numpy as jnp
from jax import lax

RANK = 256
EDGE = 32
CAP = 192
B_DEV = 16
C_DEV = 4
COLUMNS = 8
SHARDS = 32
BLOCKS = 6144
IBOX = 16
JBOX = 64
KBOX = 16
IROWS = 2048
JROWS = 16384
KROWS = 4096


def draw_blocks(key, part):
    first = jax.random.fold_in(jax.random.fold_in(key, 11), 0)
    block_shape = (BLOCKS, EDGE, EDGE * EDGE)
    base_scale = 0.5 * math.sqrt(JROWS * KROWS * IROWS / (0.31 * BLOCKS * EDGE ** 3))
    position = (jnp.arange(BLOCKS) // CAP).astype(jnp.float32) / max(SHARDS - 1, 1)
    rising = jnp.sqrt(jnp.power(5.0, position) / 2.5)
    values = jnp.clip(jax.random.normal(first, block_shape, jnp.float32), -6.0, 6.0)
    return (values * (base_scale * rising)[:, None, None]).astype(jnp.bfloat16)


def mixed_factor(key, rows):
    subkeys = jax.random.split(key, 3)
    noise = jnp.clip(jax.random.normal(subkeys[0], (rows, RANK), jnp.float32), -6.0, 6.0)
    first_mix = jax.random.uniform(subkeys[1], (RANK,), jnp.float32, 0.6, 1.0)
    second_mix = jax.random.uniform(subkeys[2], (RANK,), jnp.float32, 0.6, 1.0)
    mixed = 0.6 * noise + first_mix[None, :] * jnp.roll(noise, -1, axis=1) + second_mix[None, :] * jnp.roll(noise, -5, axis=1)
    ramp = jnp.sqrt(1.0 + 2.0 * jnp.arange(rows).astype(jnp.float32) / max(rows - 1, 1))
    return mixed * ramp[:, None] / math.sqrt(3.28 * rows)


def draw_b_factor(key, part):
    return mixed_factor(jax.random.fold_in(key, 3), JROWS)


def draw_c_factor(key, part):
    return mixed_factor(jax.random.fold_in(key, 7), KROWS)


def draw_block_count(key, part):
    first, second = jax.random.split(jax.random.fold_in(key, 5))
    counts = jax.random.randint(first, (SHARDS,), CAP // 8, CAP // 2 + 1)
    chosen = jax.random.randint(second, (), 0, SHARDS)
    return jnp.where(jnp.arange(SHARDS) == chosen, CAP, counts).astype(jnp.int32)


def with_ends(values, own_key, least, high):
    shape = values.shape
    index_at = [jax.random.randint(jax.random.fold_in(own_key, axis), (), 0, shape[axis]) for axis in range(len(shape))]
    values = values.at[tuple(index_at)].set(least)
    longest = shape.index(max(shape))
    index_at[longest] = (index_at[longest] + 1) % shape[longest]
    return values.at[tuple(index_at)].set(high)


def setup_inputs(seed: int = 0) -> dict:
    key_of = jax.random.split(jax.random.key(seed), 8)
    blocks = draw_blocks(jax.random.fold_in(key_of[7], 71), 0)
    i_index = with_ends(jax.random.randint(key_of[1], (BLOCKS,), 0, IBOX), jax.random.fold_in(key_of[1], 1), 0, IBOX - 1).astype(jnp.int32)
    j_index = with_ends(jax.random.randint(key_of[2], (BLOCKS,), 0, JBOX), jax.random.fold_in(key_of[2], 1), 0, JBOX - 1).astype(jnp.int32)
    k_index = with_ends(jax.random.randint(key_of[3], (BLOCKS,), 0, KBOX), jax.random.fold_in(key_of[3], 1), 0, KBOX - 1).astype(jnp.int32)
    block_count = draw_block_count(jax.random.fold_in(key_of[7], 71), 0)
    b_factor = draw_b_factor(jax.random.fold_in(key_of[7], 71), 0)
    c_factor = draw_c_factor(jax.random.fold_in(key_of[7], 71), 0)
    return dict(blocks=blocks, i_index=i_index, j_index=j_index, k_index=k_index, block_count=block_count, b_factor=b_factor, c_factor=c_factor)


def solve_rows(gram, right_side):
    factor_low = lax.linalg.cholesky(gram)
    halfway = lax.linalg.triangular_solve(factor_low, right_side, left_side=False, lower=True, transpose_a=True)
    return lax.linalg.triangular_solve(factor_low, halfway, left_side=False, lower=True, transpose_a=False)

def accumulate(blocks, left_table, left_global, tail_table, tail_global, target_global, live_mask, targets, first_mode):
    steps_total = blocks.shape[0] // 64
    edge_size = blocks.shape[1]
    rank_width = left_table.shape[2]

    def one_step(running, inputs):
        tensor_group, left_idx, tail_idx, target_idx, alive_row = inputs
        left_rows = left_table[left_idx].astype(jnp.float32)
        tail_rows = tail_table[tail_idx].astype(jnp.float32)
        product = (left_rows[:, :, None, :] * tail_rows[:, None, :, :]).astype(jnp.bfloat16)
        product = lax.optimization_barrier(product).astype(jnp.float32)
        tensor_wide = tensor_group.astype(jnp.float32)
        if first_mode:
            result = jnp.einsum('bim,bmr->bir', tensor_wide, product.reshape(64, edge_size * edge_size, rank_width), precision=lax.Precision.HIGHEST)
        else:
            result = jnp.einsum('bijk,bikr->bjr', tensor_wide.reshape(64, edge_size, edge_size, edge_size), product, precision=lax.Precision.HIGHEST)
        result = result * alive_row[:, None, None]
        return (running.at[target_idx].add(result), None)
    inputs = (blocks.reshape(steps_total, 64, edge_size, edge_size * edge_size), left_global.reshape(steps_total, 64), tail_global.reshape(steps_total, 64), target_global.reshape(steps_total, 64), live_mask.reshape(steps_total, 64))
    start_value = jnp.zeros((targets, edge_size, rank_width), jnp.float32)
    running, _ = lax.scan(one_step, start_value, inputs)
    return running.reshape(targets * edge_size, rank_width)

def reference(blocks, i_index, j_index, k_index, block_count, b_factor, c_factor):
    highest = lax.Precision.HIGHEST
    slot_ids = jnp.arange(BLOCKS, dtype=jnp.int32)
    device = slot_ids // CAP
    group_index = device // COLUMNS
    column = device % COLUMNS
    live_mask = (slot_ids % CAP < block_count[device]).astype(jnp.float32)
    i_global = (group_index * IBOX + i_index).astype(jnp.int32)
    j_global = ((j_index // B_DEV * COLUMNS + column) * B_DEV + j_index % B_DEV).astype(jnp.int32)
    k_global = ((k_index // C_DEV * COLUMNS + column) * C_DEV + k_index % C_DEV).astype(jnp.int32)
    gram_second = jnp.dot(b_factor.T, b_factor, precision=highest)
    gram_third = jnp.dot(c_factor.T, c_factor, precision=highest)
    b_table = b_factor.astype(jnp.bfloat16).reshape(JROWS // EDGE, EDGE, RANK)
    c_table = c_factor.astype(jnp.bfloat16).reshape(KROWS // EDGE, EDGE, RANK)
    mode_one = accumulate(blocks, b_table, j_global, c_table, k_global, i_global, live_mask, IROWS // EDGE, True)
    a_update = solve_rows(gram_second * gram_third, mode_one)
    gram_first = jnp.dot(a_update.T, a_update, precision=highest)
    col_norm = jnp.sqrt(jnp.diagonal(gram_first) + 1e-06)
    a_table = (a_update / col_norm[None, :]).astype(jnp.bfloat16).reshape(IROWS // EDGE, EDGE, RANK)
    mode_two = accumulate(blocks, a_table, i_global, c_table, k_global, j_global, live_mask, JROWS // EDGE, False)
    gram_two = gram_first / (col_norm[:, None] * col_norm[None, :]) * gram_third
    b_update = solve_rows(gram_two, mode_two)
    return (a_update, b_update)
```

```python
import functools
import jax
import jax.numpy as jnp
from jax import lax
from jax.experimental import pallas as pl
from jax.experimental.pallas import tpu as pltpu
from jax.sharding import PartitionSpec as P

HIGHEST = lax.Precision.HIGHEST
GROUP = 16
UNROLL = 2
QUARTER = 32
LANES = 128
VMEM_LIMIT = 56 * 1024 * 1024


def khatri_rao(left, tail, first):
    rows = [
        jnp.broadcast_to(left[first + t : first + t + 1, :], tail.shape).astype(jnp.bfloat16) * tail
        for t in range(8)
    ]
    return jnp.concatenate(rows, axis=0)


def product_rows(lhs_part, left, tail):
    total = None
    for q in range(4):
        term = jnp.dot(
            lhs_part(q), khatri_rao(left, tail, 8 * q), preferred_element_type=jnp.float32
        )
        total = term if total is None else total + term
    return total


def slot_loop(count, do_slot):
    base = pl.program_id(0) * GROUP
    steps = jnp.clip((count - base + UNROLL - 1) // UNROLL, 0, GROUP // UNROLL)

    def body(step, carry):
        for u in range(UNROLL):
            local = step * UNROLL + u
            do_slot(local, base + local, u)
        return carry

    lax.fori_loop(0, steps, body, 0)


def mode_one_kernel(i_ref, j_ref, k_ref, n_ref, x_ref, b_ref, c_ref, out_ref):
    @pl.when(pl.program_id(0) == 0)
    def _():
        out_ref[...] = jnp.zeros_like(out_ref)

    count = n_ref[0]

    def do_slot(local, slot, u):
        left = b_ref[pl.ds(pl.multiple_of(j_ref[slot] * 32, 32), 32), :].astype(jnp.float32)
        tail = c_ref[pl.ds(pl.multiple_of(k_ref[slot] * 32, 32), 32), :]
        result = product_rows(lambda q: x_ref[local, :, q * 256 : (q + 1) * 256], left, tail)
        alive = (slot < count).astype(jnp.float32)
        rows = pl.ds(pl.multiple_of(i_ref[slot] * 32, 32), 32)
        out_ref[rows, :] += result * alive

    slot_loop(count, do_slot)


def quarter_swap(parts):
    lane = lax.broadcasted_iota(jnp.int32, parts[0].shape, 1)
    even = (lane // QUARTER) % 2 == 0
    low = lane < 2 * QUARTER

    def pair(p, q, keep, dist):
        return (
            jnp.where(keep, p, pltpu.roll(q, dist, 1)),
            jnp.where(keep, pltpu.roll(p, LANES - dist, 1), q),
        )

    p0, p1 = pair(parts[0], parts[1], even, QUARTER)
    p2, p3 = pair(parts[2], parts[3], even, QUARTER)
    r0, r2 = pair(p0, p2, low, 2 * QUARTER)
    r1, r3 = pair(p1, p3, low, 2 * QUARTER)
    return [r0, r1, r2, r3]


def mode_two_kernel(i_ref, j_ref, k_ref, n_ref, x_ref, a_ref, c_ref, out_ref, wide):
    @pl.when(pl.program_id(0) == 0)
    def _():
        out_ref[...] = jnp.zeros_like(out_ref)

    count = n_ref[0]

    def do_slot(local, slot, u):
        for col in range(8):
            wide[u, 32 * col : 32 * col + 32, :] = x_ref[
                local, :, col * LANES : (col + 1) * LANES
            ].astype(jnp.float32)

        def lhs_part(q):
            pieces = []
            for half in range(2):
                first = q * 8 + half * 4
                parts = [wide[u, pl.ds(first + t, 8, stride=32), :] for t in range(4)]
                pieces.append(jnp.concatenate(quarter_swap(parts), axis=0).astype(jnp.bfloat16))
            return jnp.concatenate(pieces, axis=1)

        left = a_ref[pl.ds(pl.multiple_of(i_ref[slot] * 32, 32), 32), :].astype(jnp.float32)
        tail = c_ref[pl.ds(pl.multiple_of(k_ref[slot] * 32, 32), 32), :]
        result = product_rows(lhs_part, left, tail)
        alive = (slot < count).astype(jnp.float32)
        rows = pl.ds(pl.multiple_of(j_ref[slot] * 32, 32), 32)
        out_ref[rows, :] += result * alive

    slot_loop(count, do_slot)


def mode_call(kernel, scalars, blocks, left, tail, rows, scratch):
    slots, edge, width = blocks.shape
    rank = left.shape[1]
    grid_spec = pltpu.PrefetchScalarGridSpec(
        num_scalar_prefetch=4,
        grid=(slots // GROUP,),
        in_specs=[
            pl.BlockSpec((GROUP, edge, width), lambda g, *_: (g, 0, 0)),
            pl.BlockSpec(left.shape, lambda g, *_: (0, 0)),
            pl.BlockSpec(tail.shape, lambda g, *_: (0, 0)),
        ],
        out_specs=pl.BlockSpec((rows, rank), lambda g, *_: (0, 0)),
        scratch_shapes=scratch,
    )
    return pl.pallas_call(
        kernel,
        grid_spec=grid_spec,
        out_shape=jax.ShapeDtypeStruct((rows, rank), jnp.float32),
        compiler_params=pltpu.CompilerParams(vmem_limit_bytes=VMEM_LIMIT),
        cost_estimate=pl.CostEstimate(
            flops=2 * slots * edge * width * rank,
            bytes_accessed=2 * slots * edge * width,
            transcendentals=0,
        ),
    )(*scalars, blocks, left, tail)


def inverse_kernel(g_ref, out_ref):
    gram = g_ref[...]
    size = gram.shape[0]
    row = lax.broadcasted_iota(jnp.int32, gram.shape, 0)
    col = lax.broadcasted_iota(jnp.int32, gram.shape, 1)
    eye = (row == col).astype(jnp.float32)
    scale_row = lax.rsqrt(jnp.sum(gram * eye, axis=0, keepdims=True))
    scale_col = lax.rsqrt(jnp.sum(gram * eye, axis=1, keepdims=True))
    unit = gram * scale_row * scale_col
    bound = jnp.max(jnp.sum(jnp.abs(unit), axis=0, keepdims=True))

    def residual(x):
        return eye - jnp.dot(unit, x, precision=HIGHEST, preferred_element_type=jnp.float32)

    def update(x, r):
        return x + jnp.dot(x, r, precision=HIGHEST, preferred_element_type=jnp.float32)

    def more(state):
        step, worst, _, _ = state
        return jnp.logical_and(step < 60, worst > 1e-6)

    def body(state):
        step, _, x, r = state
        x = update(x, r)
        r = residual(x)
        return step + 1, jnp.sum(r * r), x, r

    x = eye * (1.0 / bound)
    r = residual(x)
    _, _, x, r = lax.while_loop(more, body, (jnp.int32(0), jnp.sum(r * r), x, r))
    out_ref[...] = update(x, r) * scale_row * scale_col


def inverse(gram):
    return pl.pallas_call(
        inverse_kernel,
        out_shape=jax.ShapeDtypeStruct(gram.shape, jnp.float32),
        in_specs=[pl.BlockSpec(memory_space=pltpu.VMEM)],
        out_specs=pl.BlockSpec(memory_space=pltpu.VMEM),
        compiler_params=pltpu.CompilerParams(vmem_limit_bytes=VMEM_LIMIT),
    )(gram)


def on_device(blocks, i_index, j_index, k_index, block_count, b_factor, c_factor):
    edge = blocks.shape[1]
    rank = b_factor.shape[1]
    gram_second, gram_third = lax.psum(
        (
            jnp.dot(b_factor.T, b_factor, precision=HIGHEST),
            jnp.dot(c_factor.T, c_factor, precision=HIGHEST),
        ),
        ("grp", "col"),
    )
    b_range = lax.all_gather(b_factor.astype(jnp.bfloat16), "grp", axis=0, tiled=True)
    c_range = lax.all_gather(c_factor.astype(jnp.bfloat16), "grp", axis=0, tiled=True)
    scalars = (i_index, j_index, k_index, block_count)
    own_rows = 2 * edge
    first_rows = own_rows * lax.axis_size("col")
    partial_one = mode_call(mode_one_kernel, scalars, blocks, b_range, c_range, first_rows, [])
    whole_sum = lax.psum(partial_one, "col")
    a_whole = jnp.dot(whole_sum, inverse(gram_second * gram_third), precision=HIGHEST)
    gram_first = lax.psum(jnp.dot(a_whole.T, a_whole, precision=HIGHEST), "grp")
    col_norm = jnp.sqrt(jnp.diagonal(gram_first) + 1e-06)
    a_range = (a_whole / col_norm[None, :]).astype(jnp.bfloat16)
    a_update = lax.dynamic_slice_in_dim(a_whole, lax.axis_index("col") * own_rows, own_rows, 0)
    gram_two = gram_first / (col_norm[:, None] * col_norm[None, :]) * gram_third
    inverse_two = inverse(gram_two)
    partial_two = mode_call(
        mode_two_kernel,
        scalars,
        blocks,
        a_range,
        c_range,
        b_range.shape[0],
        [pltpu.VMEM((UNROLL, 8 * edge, LANES), jnp.float32)],
    )
    own_two = lax.psum_scatter(partial_two, "grp", scatter_dimension=0, tiled=True)
    b_rows = jnp.dot(own_two, inverse_two, precision=HIGHEST)
    b_update = b_rows.reshape(-1, 4, 8, rank).swapaxes(1, 2).reshape(b_rows.shape)
    return (a_update, b_update)


def solution(mesh):
    return jax.shard_map(
        on_device,
        mesh=mesh,
        in_specs=(
            P(("grp", "col"), None, None),
            P(("grp", "col")),
            P(("grp", "col")),
            P(("grp", "col")),
            P(("grp", "col")),
            P(("grp", "col"), None),
            P(("grp", "col"), None),
        ),
        out_specs=(P(("grp", "col"), None), P(("grp", "col"), None)),
        check_vma=False,
    )
```

```python
import functools
import jax
import jax.numpy as jnp
from jax import lax
from jax.experimental import pallas as pl
from jax.experimental.pallas import tpu as pltpu
from jax.sharding import PartitionSpec as P

HIGHEST = lax.Precision.HIGHEST
GROUP = 16
UNROLL = 2
QUARTER = 32
LANES = 128
VMEM_LIMIT = 56 * 1024 * 1024


def khatri_rao(left, tail, first):
    rows = [
        jnp.broadcast_to(left[first + t : first + t + 1, :], tail.shape).astype(jnp.bfloat16) * tail
        for t in range(8)
    ]
    return jnp.concatenate(rows, axis=0)


def product_rows(lhs_part, left, tail):
    total = None
    for q in range(4):
        term = jnp.dot(
            lhs_part(q), khatri_rao(left, tail, 8 * q), preferred_element_type=jnp.float32
        )
        total = term if total is None else total + term
    return total


def slot_loop(count, do_slot):
    base = pl.program_id(0) * GROUP
    steps = jnp.clip((count - base + UNROLL - 1) // UNROLL, 0, GROUP // UNROLL)

    def body(step, carry):
        for u in range(UNROLL):
            local = step * UNROLL + u
            do_slot(local, base + local, u)
        return carry

    lax.fori_loop(0, steps, body, 0)


def mode_one_kernel(i_ref, j_ref, k_ref, n_ref, x_ref, b_ref, c_ref, out_ref):
    @pl.when(pl.program_id(0) == 0)
    def _():
        out_ref[...] = jnp.zeros_like(out_ref)

    count = n_ref[0]

    def do_slot(local, slot, u):
        left = b_ref[pl.ds(pl.multiple_of(j_ref[slot] * 32, 32), 32), :].astype(jnp.float32)
        tail = c_ref[pl.ds(pl.multiple_of(k_ref[slot] * 32, 32), 32), :]
        result = product_rows(lambda q: x_ref[local, :, q * 256 : (q + 1) * 256], left, tail)
        alive = (slot < count).astype(jnp.float32)
        rows = pl.ds(pl.multiple_of(i_ref[slot] * 32, 32), 32)
        out_ref[rows, :] += result * alive

    slot_loop(count, do_slot)


def quarter_swap(parts):
    lane = lax.broadcasted_iota(jnp.int32, parts[0].shape, 1)
    even = (lane // QUARTER) % 2 == 0
    low = lane < 2 * QUARTER

    def pair(p, q, keep, dist):
        return (
            jnp.where(keep, p, pltpu.roll(q, dist, 1)),
            jnp.where(keep, pltpu.roll(p, LANES - dist, 1), q),
        )

    p0, p1 = pair(parts[0], parts[1], even, QUARTER)
    p2, p3 = pair(parts[2], parts[3], even, QUARTER)
    r0, r2 = pair(p0, p2, low, 2 * QUARTER)
    r1, r3 = pair(p1, p3, low, 2 * QUARTER)
    return [r0, r1, r2, r3]


def mode_two_kernel(i_ref, j_ref, k_ref, n_ref, x_ref, a_ref, c_ref, out_ref, wide):
    @pl.when(pl.program_id(0) == 0)
    def _():
        out_ref[...] = jnp.zeros_like(out_ref)

    count = n_ref[0]

    def do_slot(local, slot, u):
        for col in range(8):
            wide[u, 32 * col : 32 * col + 32, :] = x_ref[
                local, :, col * LANES : (col + 1) * LANES
            ].astype(jnp.float32)

        def lhs_part(q):
            pieces = []
            for half in range(2):
                first = q * 8 + half * 4
                parts = [wide[u, pl.ds(first + t, 8, stride=32), :] for t in range(4)]
                pieces.append(jnp.concatenate(quarter_swap(parts), axis=0).astype(jnp.bfloat16))
            return jnp.concatenate(pieces, axis=1)

        left = a_ref[pl.ds(pl.multiple_of(i_ref[slot] * 32, 32), 32), :].astype(jnp.float32)
        tail = c_ref[pl.ds(pl.multiple_of(k_ref[slot] * 32, 32), 32), :]
        result = product_rows(lhs_part, left, tail)
        alive = (slot < count).astype(jnp.float32)
        rows = pl.ds(pl.multiple_of(j_ref[slot] * 32, 32), 32)
        out_ref[rows, :] += result * alive

    slot_loop(count, do_slot)


def mode_call(kernel, scalars, blocks, left, tail, rows, scratch):
    slots, edge, width = blocks.shape
    rank = left.shape[1]
    grid_spec = pltpu.PrefetchScalarGridSpec(
        num_scalar_prefetch=4,
        grid=(slots // GROUP,),
        in_specs=[
            pl.BlockSpec((GROUP, edge, width), lambda g, *_: (g, 0, 0)),
            pl.BlockSpec(left.shape, lambda g, *_: (0, 0)),
            pl.BlockSpec(tail.shape, lambda g, *_: (0, 0)),
        ],
        out_specs=pl.BlockSpec((rows, rank), lambda g, *_: (0, 0)),
        scratch_shapes=scratch,
    )
    return pl.pallas_call(
        kernel,
        grid_spec=grid_spec,
        out_shape=jax.ShapeDtypeStruct((rows, rank), jnp.float32),
        compiler_params=pltpu.CompilerParams(vmem_limit_bytes=VMEM_LIMIT),
        cost_estimate=pl.CostEstimate(
            flops=2 * slots * edge * width * rank,
            bytes_accessed=2 * slots * edge * width,
            transcendentals=0,
        ),
    )(*scalars, blocks, left, tail)


def inverse_kernel(g_ref, out_ref):
    gram = g_ref[...]
    size = gram.shape[0]
    row = lax.broadcasted_iota(jnp.int32, gram.shape, 0)
    col = lax.broadcasted_iota(jnp.int32, gram.shape, 1)
    eye = (row == col).astype(jnp.float32)
    scale_row = lax.rsqrt(jnp.sum(gram * eye, axis=0, keepdims=True))
    scale_col = lax.rsqrt(jnp.sum(gram * eye, axis=1, keepdims=True))
    unit = gram * scale_row * scale_col
    bound = jnp.max(jnp.sum(jnp.abs(unit), axis=0, keepdims=True))

    def residual(x):
        return eye - jnp.dot(unit, x, precision=HIGHEST, preferred_element_type=jnp.float32)

    def update(x, r):
        return x + jnp.dot(x, r, precision=HIGHEST, preferred_element_type=jnp.float32)

    def more(state):
        step, worst, _, _ = state
        return jnp.logical_and(step < 60, worst > 1e-6)

    def body(state):
        step, _, x, r = state
        x = update(x, r)
        r = residual(x)
        return step + 1, jnp.sum(r * r), x, r

    x = eye * (1.0 / bound)
    r = residual(x)
    _, _, x, r = lax.while_loop(more, body, (jnp.int32(0), jnp.sum(r * r), x, r))
    out_ref[...] = update(x, r) * scale_row * scale_col


def inverse(gram):
    return pl.pallas_call(
        inverse_kernel,
        out_shape=jax.ShapeDtypeStruct(gram.shape, jnp.float32),
        in_specs=[pl.BlockSpec(memory_space=pltpu.VMEM)],
        out_specs=pl.BlockSpec(memory_space=pltpu.VMEM),
        compiler_params=pltpu.CompilerParams(vmem_limit_bytes=VMEM_LIMIT),
    )(gram)


def me_of(shape):
    return lax.axis_index("grp"), lax.axis_index("col")


def bits_of(size):
    count = size.bit_length() - 1
    assert size == 1 << count
    return count


def flip(position, mask):
    out = position
    for t in range(mask.bit_length()):
        if (mask >> t) & 1:
            bit = (position // (1 << t)) % 2
            out = out + (1 - 2 * bit) * (1 << t)
    return out


def greet(targets):
    barrier = pltpu.get_barrier_semaphore()
    for target in targets:
        pl.semaphore_signal(barrier, inc=1, device_id=target, device_id_type=pl.DeviceIdType.MESH)
    pl.semaphore_wait(barrier, len(targets))


def send(src, dst, sems, index, target):
    copy = pltpu.make_async_remote_copy(
        src_ref=src,
        dst_ref=dst,
        send_sem=sems[0].at[index],
        recv_sem=sems[1].at[index],
        device_id=target,
        device_id_type=pl.DeviceIdType.MESH,
    )
    copy.start()
    return copy


def rows_at(first, size):
    return pl.ds(pl.multiple_of(first, 8), size)


def halve(stages, acc, landing, sems, rows):
    offset = jnp.int32(0)
    for number, (bit, target) in enumerate(stages):
        rows //= 2
        copy = send(
            acc.at[rows_at(offset + (1 - bit) * rows, rows), :],
            landing.at[pl.ds(rows, rows), :],
            sems,
            number,
            target,
        )
        offset = offset + bit * rows
        copy.wait()
        acc[rows_at(offset, rows), :] += landing[rows : 2 * rows, :]
    return offset, rows


def double(stages, full, sems, first_sem, offset, rows):
    for number, (bit, target) in reversed(list(enumerate(stages))):
        mine = full.at[rows_at(offset, rows), :]
        copy = send(mine, mine, sems, first_sem + number, target)
        copy.wait()
        offset = offset - bit * rows
        rows *= 2


def col_stages(size, first, last):
    g, c = me_of(size)
    return [((c // (1 << t)) % 2, (g, flip(c, 1 << t))) for t in range(first, min(last, bits_of(size)))]


def grp_stages(size):
    g, c = me_of(size)
    return [((g // (1 << t)) % 2, (flip(g, 1 << t), c)) for t in range(bits_of(size))]


def grp_others(size):
    g, c = me_of(size)
    return [(lax.rem(g + p, size), c) for p in range(1, size)]


def square(x):
    return lax.dot_general(
        x, x, (((0,), (0,)), ((), ())), precision=HIGHEST, preferred_element_type=jnp.float32
    )


def gather_kernel(
    grp, col, b_ref, c_ref, b_out, c_out, product_out, third_out, acc, landing, full, *sems
):
    g, c = me_of(grp)
    rank = b_ref.shape[1]
    others = grp_others(grp)
    stages = col_stages(col, 0, 1) + grp_stages(grp) + col_stages(col, 1, 64)
    greet(others + [target for _, target in col_stages(col, 0, 64)])
    pending = []
    for which, (src, out) in enumerate(((c_ref, c_out), (b_ref, b_out))):
        size = src.shape[0]
        mine = out.at[rows_at(g * size, size), :]
        mine[...] = src[...].astype(jnp.bfloat16)
        for number, target in enumerate(others):
            pending.append(send(mine, mine, sems[2:], which * (grp - 1) + number, target))
    for which, src in enumerate((b_ref, c_ref)):
        gram = square(src[...])
        for part in range(rank // LANES):
            first = (which * (rank // LANES) + part) * rank
            acc[first : first + rank, :] = gram[:, part * LANES : (part + 1) * LANES]
    offset, rows = halve(stages, acc, landing, sems, acc.shape[0])
    full[rows_at(offset, rows), :] = acc[rows_at(offset, rows), :]
    double(stages, full, sems, len(stages), offset, rows)
    half = acc.shape[0] // 2
    for part in range(rank // LANES):
        second = full[part * rank : (part + 1) * rank, :]
        third = full[half + part * rank : half + (part + 1) * rank, :]
        product_out[:, part * LANES : (part + 1) * LANES] = second * third
        third_out[:, part * LANES : (part + 1) * LANES] = third
    for copy in pending:
        copy.wait()


def reverse_bits(value, count):
    return sum(((value >> t) & 1) << (count - 1 - t) for t in range(count))


def first_factor_kernel(
    grp, col, part_ref, inverse_ref, third_ref, update_out, low_out, two_out,
    acc, landing, full, gram, piece, whole, *sems,
):
    g, c = me_of(grp)
    total = part_ref.shape[0]
    own = total // col
    count = bits_of(col)
    stages = col_stages(col, 0, 64)
    others = grp_others(grp)
    greet(others + [target for _, target in stages])
    for block in range(col):
        spot = reverse_bits(block, count) * own
        acc[spot : spot + own, :] = part_ref[block * own : (block + 1) * own, :]
    offset, rows = halve(stages, acc, landing, sems, total)
    update = jnp.dot(
        acc[rows_at(offset, rows), :],
        inverse_ref[...],
        precision=HIGHEST,
        preferred_element_type=jnp.float32,
    )
    update_out[...] = update
    full[rows_at(offset, rows), :] = update
    double(stages, full, sems, len(stages), offset, rows)
    gram[...] = square(full[...])
    size = gram.shape[0] // grp
    copies = []
    for number, target in enumerate(others):
        copies.append(
            send(gram.at[rows_at(target[0] * size, size), :], piece.at[number], sems[2:], number, target)
        )
    mine = gram[rows_at(g * size, size), :]
    for number, copy in enumerate(copies):
        copy.wait()
        mine = mine + piece[number]
    spot = whole.at[rows_at(g * size, size), :]
    spot[...] = mine
    copies = [
        send(spot, spot, sems[2:], grp - 1 + number, target) for number, target in enumerate(others)
    ]
    for copy in copies:
        copy.wait()
    gram_first = whole[...]
    row = lax.broadcasted_iota(jnp.int32, gram_first.shape, 0)
    column = lax.broadcasted_iota(jnp.int32, gram_first.shape, 1)
    diagonal = jnp.where(row == column, gram_first, 0.0)
    norm_row = jnp.sqrt(jnp.sum(diagonal, axis=0, keepdims=True) + 1e-06)
    norm_col = jnp.sqrt(jnp.sum(diagonal, axis=1, keepdims=True) + 1e-06)
    two_out[...] = gram_first / (norm_col * norm_row) * third_ref[...]
    for block in range(col):
        first = reverse_bits(block, count) * own
        low_out[block * own : (block + 1) * own, :] = (
            full[first : first + own, :] / norm_row
        ).astype(jnp.bfloat16)


def second_factor_kernel(grp, part_ref, inverse_ref, out_ref, landing, *sems):
    g, c = me_of(grp)
    count = bits_of(grp)
    own = part_ref.shape[0] // grp
    greet([target for _, target in grp_stages(grp)])
    half = part_ref.shape[1] // 2
    holding = []
    for h in range(2):
        lanes = slice(h * half, (h + 1) * half)
        holding.append(
            {m: part_ref.at[rows_at(flip(g, m) * own, own), lanes] for m in range(grp)}
        )
    spare = [0, 0]
    used = 0
    for stage in range(count):
        copies = []
        for h in range(2):
            bit = stage if h == 0 else count - 1 - stage
            target = (flip(g, 1 << bit), c)
            for m in sorted(holding[h]):
                if not (m >> bit) & 1:
                    place = landing.at[h, spare[h]]
                    spare[h] += 1
                    source = holding[h][m | (1 << bit)]
                    copies.append((h, m, bit, place, send(source, place, sems, used, target)))
                    used += 1
        for h, m, bit, place, copy in copies:
            copy.wait()
            place[...] += holding[h][m][...]
            holding[h][m] = place
            del holding[h][m | (1 << bit)]
    for h in range(2):
        out_ref[:, h * half : (h + 1) * half] = holding[h][0][...]
    rank = out_ref.shape[1]
    solved = jnp.dot(
        out_ref[...], inverse_ref[...], precision=HIGHEST, preferred_element_type=jnp.float32
    )
    out_ref[...] = solved.reshape(own // 32, 4, 8, rank).swapaxes(1, 2).reshape(own, rank)


def remote_call(kernel, number, args, outs, scratch):
    vmem = pl.BlockSpec(memory_space=pltpu.VMEM)
    return pl.pallas_call(
        kernel,
        out_shape=[jax.ShapeDtypeStruct(shape, dtype) for shape, dtype in outs],
        in_specs=[vmem] * len(args),
        out_specs=[vmem] * len(outs),
        scratch_shapes=scratch,
        compiler_params=pltpu.CompilerParams(
            collective_id=number, has_side_effects=True, vmem_limit_bytes=VMEM_LIMIT
        ),
    )(*args)


def semaphores(count):
    return [pltpu.SemaphoreType.DMA((count,))] * 2


def on_device(blocks, i_index, j_index, k_index, block_count, b_factor, c_factor):
    edge = blocks.shape[1]
    rank = b_factor.shape[1]
    grp, col = lax.axis_size("grp"), lax.axis_size("col")
    grp_bits, col_bits = bits_of(grp), bits_of(col)
    f32, bf16 = jnp.float32, jnp.bfloat16
    gram_rows = 2 * rank * (rank // LANES)
    b_range, c_range, gram_one, gram_third = remote_call(
        functools.partial(gather_kernel, grp, col),
        0,
        (b_factor, c_factor),
        [
            ((grp * b_factor.shape[0], rank), bf16),
            ((grp * c_factor.shape[0], rank), bf16),
            ((rank, rank), f32),
            ((rank, rank), f32),
        ],
        [
            pltpu.VMEM((gram_rows, LANES), f32),
            pltpu.VMEM((gram_rows, LANES), f32),
            pltpu.VMEM((gram_rows, LANES), f32),
        ]
        + semaphores(2 * (grp_bits + col_bits))
        + semaphores(2 * (grp - 1)),
    )
    scalars = (i_index, j_index, k_index, block_count)
    own_rows = 2 * edge
    first_rows = own_rows * col
    partial_one = mode_call(mode_one_kernel, scalars, blocks, b_range, c_range, first_rows, [])
    a_update, a_range, gram_two = remote_call(
        functools.partial(first_factor_kernel, grp, col),
        1,
        (partial_one, inverse(gram_one), gram_third),
        [((own_rows, rank), f32), ((first_rows, rank), bf16), ((rank, rank), f32)],
        [
            pltpu.VMEM((first_rows, rank), f32),
            pltpu.VMEM((first_rows, rank), f32),
            pltpu.VMEM((first_rows, rank), f32),
            pltpu.VMEM((rank, rank), f32),
            pltpu.VMEM((grp - 1, rank // grp, rank), f32),
            pltpu.VMEM((rank, rank), f32),
        ]
        + semaphores(2 * col_bits)
        + semaphores(2 * (grp - 1)),
    )
    inverse_two = inverse(gram_two)
    second_rows = b_range.shape[0]
    partial_two = mode_call(
        mode_two_kernel,
        scalars,
        blocks,
        a_range,
        c_range,
        second_rows,
        [pltpu.VMEM((UNROLL, 8 * edge, LANES), f32)],
    )
    (b_update,) = remote_call(
        functools.partial(second_factor_kernel, grp),
        2,
        (partial_two, inverse_two),
        [((second_rows // grp, rank), f32)],
        [pltpu.VMEM((2, grp - 1, second_rows // grp, rank // 2), f32)] + semaphores(2 * (grp - 1)),
    )
    return (a_update, b_update)


def solution(mesh):
    return jax.shard_map(
        on_device,
        mesh=mesh,
        in_specs=(
            P(("grp", "col"), None, None),
            P(("grp", "col")),
            P(("grp", "col")),
            P(("grp", "col")),
            P(("grp", "col")),
            P(("grp", "col"), None),
            P(("grp", "col"), None),
        ),
        out_specs=(P(("grp", "col"), None), P(("grp", "col"), None)),
        check_vma=False,
    )
```

```python
import functools
import jax
import jax.numpy as jnp
from jax import lax
from jax.experimental import pallas as pl
from jax.experimental.pallas import tpu as pltpu
from jax.sharding import PartitionSpec as P

HIGHEST = lax.Precision.HIGHEST
GROUP = 16
UNROLL = 4
QUARTER = 32
LANES = 128
VMEM_LIMIT = 56 * 1024 * 1024


def khatri_rao(left, tail, first):
    rows = [
        jnp.broadcast_to(left[first + t : first + t + 1, :], tail.shape).astype(jnp.bfloat16) * tail
        for t in range(8)
    ]
    return jnp.concatenate(rows, axis=0)


def product_rows(lhs_part, left, tail):
    total = None
    for q in range(4):
        term = jnp.dot(
            lhs_part(q), khatri_rao(left, tail, 8 * q), preferred_element_type=jnp.float32
        )
        total = term if total is None else total + term
    return total


def slot_loop(count, do_slot):
    base = pl.program_id(0) * GROUP
    steps = jnp.clip((count - base + UNROLL - 1) // UNROLL, 0, GROUP // UNROLL)

    def body(step, carry):
        for u in range(UNROLL):
            local = step * UNROLL + u
            do_slot(local, base + local, u)
        return carry

    lax.fori_loop(0, steps, body, 0)


def mode_one_kernel(i_ref, j_ref, k_ref, n_ref, x_ref, b_ref, c_ref, out_ref):
    @pl.when(pl.program_id(0) == 0)
    def _():
        out_ref[...] = jnp.zeros_like(out_ref)

    count = n_ref[0]

    def do_slot(local, slot, u):
        left = b_ref[pl.ds(pl.multiple_of(j_ref[slot] * 32, 32), 32), :].astype(jnp.float32)
        tail = c_ref[pl.ds(pl.multiple_of(k_ref[slot] * 32, 32), 32), :]
        result = product_rows(lambda q: x_ref[local, :, q * 256 : (q + 1) * 256], left, tail)
        alive = (slot < count).astype(jnp.float32)
        rows = pl.ds(pl.multiple_of(i_ref[slot] * 32, 32), 32)
        out_ref[rows, :] += result * alive

    slot_loop(count, do_slot)


def quarter_swap(parts):
    lane = lax.broadcasted_iota(jnp.int32, parts[0].shape, 1)
    even = (lane // QUARTER) % 2 == 0
    low = lane < 2 * QUARTER

    def pair(p, q, keep, dist):
        return (
            jnp.where(keep, p, pltpu.roll(q, dist, 1)),
            jnp.where(keep, pltpu.roll(p, LANES - dist, 1), q),
        )

    p0, p1 = pair(parts[0], parts[1], even, QUARTER)
    p2, p3 = pair(parts[2], parts[3], even, QUARTER)
    r0, r2 = pair(p0, p2, low, 2 * QUARTER)
    r1, r3 = pair(p1, p3, low, 2 * QUARTER)
    return [r0, r1, r2, r3]


def mode_two_kernel(i_ref, j_ref, k_ref, n_ref, x_ref, a_ref, c_ref, out_ref, wide):
    @pl.when(pl.program_id(0) == 0)
    def _():
        out_ref[...] = jnp.zeros_like(out_ref)

    count = n_ref[0]

    def do_slot(local, slot, u):
        for col in range(8):
            wide[u, 32 * col : 32 * col + 32, :] = x_ref[
                local, :, col * LANES : (col + 1) * LANES
            ].astype(jnp.float32)

        def lhs_part(q):
            pieces = []
            for half in range(2):
                first = q * 8 + half * 4
                parts = [wide[u, pl.ds(first + t, 8, stride=32), :] for t in range(4)]
                pieces.append(jnp.concatenate(quarter_swap(parts), axis=0).astype(jnp.bfloat16))
            return jnp.concatenate(pieces, axis=1)

        left = a_ref[pl.ds(pl.multiple_of(i_ref[slot] * 32, 32), 32), :].astype(jnp.float32)
        tail = c_ref[pl.ds(pl.multiple_of(k_ref[slot] * 32, 32), 32), :]
        result = product_rows(lhs_part, left, tail)
        alive = (slot < count).astype(jnp.float32)
        rows = pl.ds(pl.multiple_of(j_ref[slot] * 32, 32), 32)
        out_ref[rows, :] += result * alive

    slot_loop(count, do_slot)


def mode_call(kernel, scalars, blocks, left, tail, rows, scratch):
    slots, edge, width = blocks.shape
    rank = left.shape[1]
    grid_spec = pltpu.PrefetchScalarGridSpec(
        num_scalar_prefetch=4,
        grid=(slots // GROUP,),
        in_specs=[
            pl.BlockSpec((GROUP, edge, width), lambda g, *_: (g, 0, 0)),
            pl.BlockSpec(left.shape, lambda g, *_: (0, 0)),
            pl.BlockSpec(tail.shape, lambda g, *_: (0, 0)),
        ],
        out_specs=pl.BlockSpec((rows, rank), lambda g, *_: (0, 0)),
        scratch_shapes=scratch,
    )
    return pl.pallas_call(
        kernel,
        grid_spec=grid_spec,
        out_shape=jax.ShapeDtypeStruct((rows, rank), jnp.float32),
        compiler_params=pltpu.CompilerParams(vmem_limit_bytes=VMEM_LIMIT),
        cost_estimate=pl.CostEstimate(
            flops=2 * slots * edge * width * rank,
            bytes_accessed=2 * slots * edge * width,
            transcendentals=0,
        ),
    )(*scalars, blocks, left, tail)


def inverse_kernel(g_ref, out_ref):
    gram = g_ref[...]
    row = lax.broadcasted_iota(jnp.int32, gram.shape, 0)
    col = lax.broadcasted_iota(jnp.int32, gram.shape, 1)
    eye = (row == col).astype(jnp.float32)
    scale_row = lax.rsqrt(jnp.sum(gram * eye, axis=0, keepdims=True))
    scale_col = lax.rsqrt(jnp.sum(gram * eye, axis=1, keepdims=True))
    unit = gram * scale_row * scale_col
    bound = 1.0 / jnp.max(jnp.sum(jnp.abs(unit), axis=0, keepdims=True))

    def residual(x):
        return eye - jnp.dot(unit, x, precision=HIGHEST, preferred_element_type=jnp.float32)

    def update(x, r):
        return x + jnp.dot(x, r, precision=HIGHEST, preferred_element_type=jnp.float32)

    unit_low = unit.astype(jnp.bfloat16)

    def body_low(state):
        step, _, x, r = state
        x = x + jnp.dot(
            x.astype(jnp.bfloat16), r.astype(jnp.bfloat16), preferred_element_type=jnp.float32
        )
        r = eye - jnp.dot(unit_low, x.astype(jnp.bfloat16), preferred_element_type=jnp.float32)
        return step + 1, jnp.sum(r * r), x, r

    def body(state):
        step, _, x, r = state
        x = update(x, r)
        r = residual(x)
        return step + 1, jnp.sum(r * r), x, r

    def more_low(state):
        return jnp.logical_and(state[0] < 16, state[1] > 0.01)

    def more(state):
        return jnp.logical_and(state[0] < 60, state[1] > 1e-6)

    start = eye * bound
    start_r = eye - unit * bound
    _, _, x, _ = lax.while_loop(
        more_low, body_low, (jnp.int32(0), jnp.sum(start_r * start_r), start, start_r)
    )
    r = residual(x)
    good = jnp.sum(r * r) < 0.25
    x = jnp.where(good, x, start)
    r = jnp.where(good, r, start_r)
    _, _, x, r = lax.while_loop(more, body, (jnp.int32(0), jnp.sum(r * r), x, r))
    out_ref[...] = update(x, r) * scale_row * scale_col


def inverse(gram):
    return pl.pallas_call(
        inverse_kernel,
        out_shape=jax.ShapeDtypeStruct(gram.shape, jnp.float32),
        in_specs=[pl.BlockSpec(memory_space=pltpu.VMEM)],
        out_specs=pl.BlockSpec(memory_space=pltpu.VMEM),
        compiler_params=pltpu.CompilerParams(vmem_limit_bytes=VMEM_LIMIT),
    )(gram)


def me_of(shape):
    return lax.axis_index("grp"), lax.axis_index("col")


def bits_of(size):
    count = size.bit_length() - 1
    assert size == 1 << count
    return count


def flip(position, mask):
    out = position
    for t in range(mask.bit_length()):
        if (mask >> t) & 1:
            bit = (position // (1 << t)) % 2
            out = out + (1 - 2 * bit) * (1 << t)
    return out


def greet(targets):
    barrier = pltpu.get_barrier_semaphore()
    for target in targets:
        pl.semaphore_signal(barrier, inc=1, device_id=target, device_id_type=pl.DeviceIdType.MESH)
    pl.semaphore_wait(barrier, len(targets))


def send(src, dst, sems, index, target):
    copy = pltpu.make_async_remote_copy(
        src_ref=src,
        dst_ref=dst,
        send_sem=sems[0].at[index],
        recv_sem=sems[1].at[index],
        device_id=target,
        device_id_type=pl.DeviceIdType.MESH,
    )
    copy.start()
    return copy


def rows_at(first, size):
    return pl.ds(pl.multiple_of(first, 8), size)


def scatter_sum(group, acc, landing, sems, first, offset, rows):
    index, targets = group
    size = len(targets) + 1
    chunk = rows // size
    copies = []
    for number, (other, target) in enumerate(targets):
        place = landing.at[pl.ds(rows - (number + 1) * chunk, chunk), :]
        copies.append(
            send(acc.at[rows_at(offset + other * chunk, chunk), :], place, sems, first + number, target)
        )
    offset = offset + index * chunk
    for number, copy in enumerate(copies):
        copy.wait()
        low = rows - (number + 1) * chunk
        acc[rows_at(offset, chunk), :] += landing[low : low + chunk, :]
    return offset, chunk


def spread(group, full, sems, first, offset, rows):
    index, targets = group
    copies = []
    mine = full.at[rows_at(offset, rows), :]
    for number, (_, target) in enumerate(targets):
        copies.append(send(mine, mine, sems, first + number, target))
    for copy in copies:
        copy.wait()
    return offset - index * rows, rows * (len(targets) + 1)


def scatter_all(groups, acc, landing, sems):
    offset, rows, first = jnp.int32(0), acc.shape[0], 0
    for group in groups:
        offset, rows = scatter_sum(group, acc, landing, sems, first, offset, rows)
        first += len(group[1])
    return offset, rows


def spread_all(groups, full, sems, offset, rows):
    first = sum(len(group[1]) for group in groups)
    for group in reversed(groups):
        offset, rows = spread(group, full, sems, first, offset, rows)
        first += len(group[1])


def core_group():
    g, c = lax.axis_index("grp"), lax.axis_index("col")
    core = lax.rem(c, 2)
    return core, [(1 - core, (g, c + 1 - 2 * core))]


def chip_group(col):
    g, c = lax.axis_index("grp"), lax.axis_index("col")
    chips, core, chip = col // 2, lax.rem(c, 2), c // 2
    others = [lax.rem(chip + p, chips) for p in range(1, chips)]
    return chip, [(other, (g, other * 2 + core)) for other in others]


def grp_group(grp):
    g, c = lax.axis_index("grp"), lax.axis_index("col")
    others = [lax.rem(g + p, grp) for p in range(1, grp)]
    return g, [(other, (other, c)) for other in others]


def grp_stages(size):
    g, c = me_of(size)
    return [((g // (1 << t)) % 2, (flip(g, 1 << t), c)) for t in range(bits_of(size))]


def targets_of(groups):
    return [target for _, targets in groups for _, target in targets]


def square(x):
    high = x.astype(jnp.bfloat16)
    low = (x - high.astype(jnp.float32)).astype(jnp.bfloat16)

    def dot(p, q):
        return lax.dot_general(
            p, q, (((0,), (0,)), ((), ())), preferred_element_type=jnp.float32
        )

    cross = dot(high, low)
    return dot(high, high) + (cross + cross.T)


def gather_kernel(
    grp, col, b_ref, c_ref, b_out, c_out, product_out, third_out, acc, landing, full, *sems
):
    g, c = me_of(grp)
    rank = b_ref.shape[1]
    groups = [core_group(), chip_group(col), grp_group(grp)]
    others = targets_of(groups[2:])
    greet(targets_of(groups))
    pending = []
    for which, (src, out) in enumerate(((c_ref, c_out), (b_ref, b_out))):
        size = src.shape[0]
        mine = out.at[rows_at(g * size, size), :]
        mine[...] = src[...].astype(jnp.bfloat16)
        for number, target in enumerate(others):
            pending.append(send(mine, mine, sems[2:], which * (grp - 1) + number, target))
    for which, src in enumerate((b_ref, c_ref)):
        gram = square(src[...])
        for part in range(rank // LANES):
            first = (which * (rank // LANES) + part) * rank
            acc[first : first + rank, :] = gram[:, part * LANES : (part + 1) * LANES]
    offset, rows = scatter_all(groups, acc, landing, sems)
    full[rows_at(offset, rows), :] = acc[rows_at(offset, rows), :]
    spread_all(groups, full, sems, offset, rows)
    half = acc.shape[0] // 2
    for part in range(rank // LANES):
        second = full[part * rank : (part + 1) * rank, :]
        third = full[half + part * rank : half + (part + 1) * rank, :]
        product_out[:, part * LANES : (part + 1) * LANES] = second * third
        third_out[:, part * LANES : (part + 1) * LANES] = third
    for copy in pending:
        copy.wait()


def first_factor_kernel(
    grp, col, part_ref, inverse_ref, third_ref, update_out, low_out, two_out,
    acc, landing, full, gram, piece, whole, *sems,
):
    g, c = me_of(grp)
    total = part_ref.shape[0]
    own = total // col
    groups = [core_group(), chip_group(col)]
    others = targets_of([grp_group(grp)])
    greet(others + targets_of(groups))
    for block in range(col):
        spot = (block % 2 * (col // 2) + block // 2) * own
        acc[spot : spot + own, :] = part_ref[block * own : (block + 1) * own, :]
    offset, rows = scatter_all(groups, acc, landing, sems)
    update = jnp.dot(
        acc[rows_at(offset, rows), :],
        inverse_ref[...],
        precision=HIGHEST,
        preferred_element_type=jnp.float32,
    )
    update_out[...] = update
    full[rows_at(offset, rows), :] = update
    spread_all(groups, full, sems, offset, rows)
    gram[...] = square(full[...])
    size = gram.shape[0] // grp
    copies = []
    for number, target in enumerate(others):
        copies.append(
            send(gram.at[rows_at(target[0] * size, size), :], piece.at[number], sems[2:], number, target)
        )
    mine = gram[rows_at(g * size, size), :]
    for number, copy in enumerate(copies):
        copy.wait()
        mine = mine + piece[number]
    spot = whole.at[rows_at(g * size, size), :]
    spot[...] = mine
    copies = [
        send(spot, spot, sems[2:], grp - 1 + number, target) for number, target in enumerate(others)
    ]
    for copy in copies:
        copy.wait()
    gram_first = whole[...]
    row = lax.broadcasted_iota(jnp.int32, gram_first.shape, 0)
    column = lax.broadcasted_iota(jnp.int32, gram_first.shape, 1)
    diagonal = jnp.where(row == column, gram_first, 0.0)
    norm_row = jnp.sqrt(jnp.sum(diagonal, axis=0, keepdims=True) + 1e-06)
    norm_col = jnp.sqrt(jnp.sum(diagonal, axis=1, keepdims=True) + 1e-06)
    two_out[...] = gram_first / (norm_col * norm_row) * third_ref[...]
    for block in range(col):
        first = (block % 2 * (col // 2) + block // 2) * own
        low_out[block * own : (block + 1) * own, :] = (
            full[first : first + own, :] / norm_row
        ).astype(jnp.bfloat16)


def second_factor_kernel(grp, part_ref, inverse_ref, out_ref, landing, *sems):
    g, c = me_of(grp)
    count = bits_of(grp)
    own = part_ref.shape[0] // grp
    greet([target for _, target in grp_stages(grp)])
    half = part_ref.shape[1] // 2
    holding = []
    for h in range(2):
        lanes = slice(h * half, (h + 1) * half)
        holding.append(
            {m: part_ref.at[rows_at(flip(g, m) * own, own), lanes] for m in range(grp)}
        )
    spare = [0, 0]
    used = 0
    for stage in range(count):
        copies = []
        for h in range(2):
            bit = stage if h == 0 else count - 1 - stage
            target = (flip(g, 1 << bit), c)
            for m in sorted(holding[h]):
                if not (m >> bit) & 1:
                    place = landing.at[h, spare[h]]
                    spare[h] += 1
                    source = holding[h][m | (1 << bit)]
                    copies.append((h, m, bit, place, send(source, place, sems, used, target)))
                    used += 1
        for h, m, bit, place, copy in copies:
            copy.wait()
            place[...] += holding[h][m][...]
            holding[h][m] = place
            del holding[h][m | (1 << bit)]
    for h in range(2):
        out_ref[:, h * half : (h + 1) * half] = holding[h][0][...]
    rank = out_ref.shape[1]
    solved = jnp.dot(
        out_ref[...], inverse_ref[...], precision=HIGHEST, preferred_element_type=jnp.float32
    )
    out_ref[...] = solved.reshape(own // 32, 4, 8, rank).swapaxes(1, 2).reshape(own, rank)


def remote_call(kernel, number, args, outs, scratch):
    vmem = pl.BlockSpec(memory_space=pltpu.VMEM)
    return pl.pallas_call(
        kernel,
        out_shape=[jax.ShapeDtypeStruct(shape, dtype) for shape, dtype in outs],
        in_specs=[vmem] * len(args),
        out_specs=[vmem] * len(outs),
        scratch_shapes=scratch,
        compiler_params=pltpu.CompilerParams(
            collective_id=number, has_side_effects=True, vmem_limit_bytes=VMEM_LIMIT
        ),
    )(*args)


def semaphores(count):
    return [pltpu.SemaphoreType.DMA((count,))] * 2


def on_device(blocks, i_index, j_index, k_index, block_count, b_factor, c_factor):
    edge = blocks.shape[1]
    rank = b_factor.shape[1]
    grp, col = lax.axis_size("grp"), lax.axis_size("col")
    col_links = col // 2
    f32, bf16 = jnp.float32, jnp.bfloat16
    gram_rows = 2 * rank * (rank // LANES)
    b_range, c_range, gram_one, gram_third = remote_call(
        functools.partial(gather_kernel, grp, col),
        0,
        (b_factor, c_factor),
        [
            ((grp * b_factor.shape[0], rank), bf16),
            ((grp * c_factor.shape[0], rank), bf16),
            ((rank, rank), f32),
            ((rank, rank), f32),
        ],
        [
            pltpu.VMEM((gram_rows, LANES), f32),
            pltpu.VMEM((gram_rows, LANES), f32),
            pltpu.VMEM((gram_rows, LANES), f32),
        ]
        + semaphores(2 * (col_links + grp - 1))
        + semaphores(2 * (grp - 1)),
    )
    scalars = (i_index, j_index, k_index, block_count)
    own_rows = 2 * edge
    first_rows = own_rows * col
    partial_one = mode_call(mode_one_kernel, scalars, blocks, b_range, c_range, first_rows, [])
    a_update, a_range, gram_two = remote_call(
        functools.partial(first_factor_kernel, grp, col),
        1,
        (partial_one, inverse(gram_one), gram_third),
        [((own_rows, rank), f32), ((first_rows, rank), bf16), ((rank, rank), f32)],
        [
            pltpu.VMEM((first_rows, rank), f32),
            pltpu.VMEM((first_rows, rank), f32),
            pltpu.VMEM((first_rows, rank), f32),
            pltpu.VMEM((rank, rank), f32),
            pltpu.VMEM((grp - 1, rank // grp, rank), f32),
            pltpu.VMEM((rank, rank), f32),
        ]
        + semaphores(2 * col_links)
        + semaphores(2 * (grp - 1)),
    )
    inverse_two = inverse(gram_two)
    second_rows = b_range.shape[0]
    partial_two = mode_call(
        mode_two_kernel,
        scalars,
        blocks,
        a_range,
        c_range,
        second_rows,
        [pltpu.VMEM((UNROLL, 8 * edge, LANES), f32)],
    )
    (b_update,) = remote_call(
        functools.partial(second_factor_kernel, grp),
        2,
        (partial_two, inverse_two),
        [((second_rows // grp, rank), f32)],
        [pltpu.VMEM((2, grp - 1, second_rows // grp, rank // 2), f32)] + semaphores(2 * (grp - 1)),
    )
    return (a_update, b_update)


def solution(mesh):
    return jax.shard_map(
        on_device,
        mesh=mesh,
        in_specs=(
            P(("grp", "col"), None, None),
            P(("grp", "col")),
            P(("grp", "col")),
            P(("grp", "col")),
            P(("grp", "col")),
            P(("grp", "col"), None),
            P(("grp", "col"), None),
        ),
        out_specs=(P(("grp", "col"), None), P(("grp", "col"), None)),
        check_vma=False,
    )
```

```python
import functools
import jax
import jax.numpy as jnp
from jax import lax
from jax.experimental import pallas as pl
from jax.experimental.pallas import tpu as pltpu
from jax.sharding import PartitionSpec as P

HIGHEST = lax.Precision.HIGHEST
GROUP = 16
UNROLL = 8
QUARTER = 32
LANES = 128
VMEM_LIMIT = 56 * 1024 * 1024


def khatri_rao(left, tail, first):
    rows = [
        jnp.broadcast_to(left[first + t : first + t + 1, :], tail.shape).astype(jnp.bfloat16) * tail
        for t in range(8)
    ]
    return jnp.concatenate(rows, axis=0)


def product_rows(lhs_part, left, tail):
    total = None
    for q in range(4):
        term = jnp.dot(
            lhs_part(q), khatri_rao(left, tail, 8 * q), preferred_element_type=jnp.float32
        )
        total = term if total is None else total + term
    return total


def slot_loop(count, do_slot):
    base = pl.program_id(0) * GROUP
    steps = jnp.clip((count - base + UNROLL - 1) // UNROLL, 0, GROUP // UNROLL)

    def body(step, carry):
        for u in range(UNROLL):
            local = step * UNROLL + u
            do_slot(local, base + local, u)
        return carry

    lax.fori_loop(0, steps, body, 0)


def mode_one_kernel(i_ref, j_ref, k_ref, n_ref, x_ref, b_ref, c_ref, out_ref):
    @pl.when(pl.program_id(0) == 0)
    def _():
        out_ref[...] = jnp.zeros_like(out_ref)

    count = n_ref[0]

    def do_slot(local, slot, u):
        left = b_ref[pl.ds(pl.multiple_of(j_ref[slot] * 32, 32), 32), :].astype(jnp.float32)
        tail = c_ref[pl.ds(pl.multiple_of(k_ref[slot] * 32, 32), 32), :]
        result = product_rows(lambda q: x_ref[local, :, q * 256 : (q + 1) * 256], left, tail)
        alive = (slot < count).astype(jnp.float32)
        rows = pl.ds(pl.multiple_of(i_ref[slot] * 32, 32), 32)
        out_ref[rows, :] += result * alive

    slot_loop(count, do_slot)


def quarter_swap(parts):
    lane = lax.broadcasted_iota(jnp.int32, parts[0].shape, 1)
    even = (lane // QUARTER) % 2 == 0
    low = lane < 2 * QUARTER

    def pair(p, q, keep, dist):
        return (
            jnp.where(keep, p, pltpu.roll(q, dist, 1)),
            jnp.where(keep, pltpu.roll(p, LANES - dist, 1), q),
        )

    p0, p1 = pair(parts[0], parts[1], even, QUARTER)
    p2, p3 = pair(parts[2], parts[3], even, QUARTER)
    r0, r2 = pair(p0, p2, low, 2 * QUARTER)
    r1, r3 = pair(p1, p3, low, 2 * QUARTER)
    return [r0, r1, r2, r3]


def mode_two_kernel(i_ref, j_ref, k_ref, n_ref, x_ref, a_ref, c_ref, out_ref, wide):
    @pl.when(pl.program_id(0) == 0)
    def _():
        out_ref[...] = jnp.zeros_like(out_ref)

    count = n_ref[0]

    def do_slot(local, slot, u):
        for col in range(8):
            wide[u, 32 * col : 32 * col + 32, :] = x_ref[
                local, :, col * LANES : (col + 1) * LANES
            ].astype(jnp.float32)

        def lhs_part(q):
            pieces = []
            for half in range(2):
                first = q * 8 + half * 4
                parts = [wide[u, pl.ds(first + t, 8, stride=32), :] for t in range(4)]
                pieces.append(jnp.concatenate(quarter_swap(parts), axis=0).astype(jnp.bfloat16))
            return jnp.concatenate(pieces, axis=1)

        left = a_ref[pl.ds(pl.multiple_of(i_ref[slot] * 32, 32), 32), :].astype(jnp.float32)
        tail = c_ref[pl.ds(pl.multiple_of(k_ref[slot] * 32, 32), 32), :]
        result = product_rows(lhs_part, left, tail)
        alive = (slot < count).astype(jnp.float32)
        rows = pl.ds(pl.multiple_of(j_ref[slot] * 32, 32), 32)
        out_ref[rows, :] += result * alive

    slot_loop(count, do_slot)


def mode_call(kernel, scalars, blocks, left, tail, rows, scratch):
    slots, edge, width = blocks.shape
    rank = left.shape[1]
    grid_spec = pltpu.PrefetchScalarGridSpec(
        num_scalar_prefetch=4,
        grid=(slots // GROUP,),
        in_specs=[
            pl.BlockSpec((GROUP, edge, width), lambda g, *_: (g, 0, 0)),
            pl.BlockSpec(left.shape, lambda g, *_: (0, 0)),
            pl.BlockSpec(tail.shape, lambda g, *_: (0, 0)),
        ],
        out_specs=pl.BlockSpec((rows, rank), lambda g, *_: (0, 0)),
        scratch_shapes=scratch,
    )
    return pl.pallas_call(
        kernel,
        grid_spec=grid_spec,
        out_shape=jax.ShapeDtypeStruct((rows, rank), jnp.float32),
        compiler_params=pltpu.CompilerParams(vmem_limit_bytes=VMEM_LIMIT),
        cost_estimate=pl.CostEstimate(
            flops=2 * slots * edge * width * rank,
            bytes_accessed=2 * slots * edge * width,
            transcendentals=0,
        ),
    )(*scalars, blocks, left, tail)


def inverse_kernel(lead_ref, g_ref, out_ref):
    @pl.when(lead_ref[0] == 0)
    def _():
        out_ref[...] = jnp.zeros_like(out_ref)

    @pl.when(lead_ref[0] != 0)
    def _():
        out_ref[...] = newton_inverse(g_ref[...])


def newton_inverse(gram):
    row = lax.broadcasted_iota(jnp.int32, gram.shape, 0)
    col = lax.broadcasted_iota(jnp.int32, gram.shape, 1)
    eye = (row == col).astype(jnp.float32)
    scale_row = lax.rsqrt(jnp.sum(gram * eye, axis=0, keepdims=True))
    scale_col = lax.rsqrt(jnp.sum(gram * eye, axis=1, keepdims=True))
    unit = gram * scale_row * scale_col
    bound = 1.0 / jnp.max(jnp.sum(jnp.abs(unit), axis=0, keepdims=True))

    def residual(x):
        return eye - jnp.dot(unit, x, precision=HIGHEST, preferred_element_type=jnp.float32)

    def update(x, r):
        return x + jnp.dot(x, r, precision=HIGHEST, preferred_element_type=jnp.float32)

    unit_low = unit.astype(jnp.bfloat16)

    def body_low(state):
        step, _, x, r = state
        x = x + jnp.dot(
            x.astype(jnp.bfloat16), r.astype(jnp.bfloat16), preferred_element_type=jnp.float32
        )
        r = eye - jnp.dot(unit_low, x.astype(jnp.bfloat16), preferred_element_type=jnp.float32)
        return step + 1, jnp.sum(r * r), x, r

    def body(state):
        step, _, x, r = state
        x = update(x, r)
        r = residual(x)
        return step + 1, jnp.sum(r * r), x, r

    def more_low(state):
        return jnp.logical_and(state[0] < 16, state[1] > 0.01)

    def more(state):
        return jnp.logical_and(state[0] < 60, state[1] > 1e-6)

    start = eye * bound
    start_r = eye - unit * bound
    _, _, x, _ = lax.while_loop(
        more_low, body_low, (jnp.int32(0), jnp.sum(start_r * start_r), start, start_r)
    )
    r = residual(x)
    good = jnp.sum(r * r) < 0.25
    x = jnp.where(good, x, start)
    r = jnp.where(good, r, start_r)
    _, _, x, r = lax.while_loop(more, body, (jnp.int32(0), jnp.sum(r * r), x, r))
    return update(x, r) * scale_row * scale_col


def inverse(lead, gram):
    return pl.pallas_call(
        inverse_kernel,
        out_shape=jax.ShapeDtypeStruct(gram.shape, jnp.float32),
        in_specs=[
            pl.BlockSpec(memory_space=pltpu.SMEM),
            pl.BlockSpec(memory_space=pltpu.VMEM),
        ],
        out_specs=pl.BlockSpec(memory_space=pltpu.VMEM),
        compiler_params=pltpu.CompilerParams(vmem_limit_bytes=VMEM_LIMIT),
    )(lead, gram)


def solve_kernel(sum_ref, mine_ref, other_ref, out_ref):
    own, rank = sum_ref.shape
    solved = jnp.dot(
        sum_ref[...],
        mine_ref[...] + other_ref[...],
        precision=HIGHEST,
        preferred_element_type=jnp.float32,
    )
    out_ref[...] = solved.reshape(own // 32, 4, 8, rank).swapaxes(1, 2).reshape(own, rank)


def me_of(shape):
    return lax.axis_index("grp"), lax.axis_index("col")


def bits_of(size):
    count = size.bit_length() - 1
    assert size == 1 << count
    return count


def flip(position, mask):
    out = position
    for t in range(mask.bit_length()):
        if (mask >> t) & 1:
            bit = (position // (1 << t)) % 2
            out = out + (1 - 2 * bit) * (1 << t)
    return out


def greet(targets):
    barrier = pltpu.get_barrier_semaphore()
    for target in targets:
        pl.semaphore_signal(barrier, inc=1, device_id=target, device_id_type=pl.DeviceIdType.MESH)
    pl.semaphore_wait(barrier, len(targets))


def send(src, dst, sems, index, target):
    copy = pltpu.make_async_remote_copy(
        src_ref=src,
        dst_ref=dst,
        send_sem=sems[0].at[index],
        recv_sem=sems[1].at[index],
        device_id=target,
        device_id_type=pl.DeviceIdType.MESH,
    )
    copy.start()
    return copy


def rows_at(first, size):
    return pl.ds(pl.multiple_of(first, 8), size)


def scatter_sum(group, acc, landing, sems, first, offset, rows):
    index, targets = group
    size = len(targets) + 1
    chunk = rows // size
    copies = []
    for number, (other, target) in enumerate(targets):
        place = landing.at[pl.ds(rows - (number + 1) * chunk, chunk), :]
        copies.append(
            send(acc.at[rows_at(offset + other * chunk, chunk), :], place, sems, first + number, target)
        )
    offset = offset + index * chunk
    for number, copy in enumerate(copies):
        copy.wait()
        low = rows - (number + 1) * chunk
        acc[rows_at(offset, chunk), :] += landing[low : low + chunk, :]
    return offset, chunk


def spread(group, full, sems, first, offset, rows):
    index, targets = group
    copies = []
    mine = full.at[rows_at(offset, rows), :]
    for number, (_, target) in enumerate(targets):
        copies.append(send(mine, mine, sems, first + number, target))
    for copy in copies:
        copy.wait()
    return offset - index * rows, rows * (len(targets) + 1)


def scatter_all(groups, acc, landing, sems):
    offset, rows, first = jnp.int32(0), acc.shape[0], 0
    for group in groups:
        offset, rows = scatter_sum(group, acc, landing, sems, first, offset, rows)
        first += len(group[1])
    return offset, rows


def spread_all(groups, full, sems, offset, rows):
    first = sum(len(group[1]) for group in groups)
    for group in reversed(groups):
        offset, rows = spread(group, full, sems, first, offset, rows)
        first += len(group[1])


def core_group():
    g, c = lax.axis_index("grp"), lax.axis_index("col")
    core = lax.rem(c, 2)
    return core, [(1 - core, (g, c + 1 - 2 * core))]


def chip_group(col):
    g, c = lax.axis_index("grp"), lax.axis_index("col")
    chips, core, chip = col // 2, lax.rem(c, 2), c // 2
    others = [lax.rem(chip + p, chips) for p in range(1, chips)]
    return chip, [(other, (g, other * 2 + core)) for other in others]


def grp_group(grp):
    g, c = lax.axis_index("grp"), lax.axis_index("col")
    others = [lax.rem(g + p, grp) for p in range(1, grp)]
    return g, [(other, (other, c)) for other in others]


def grp_stages(size):
    g, c = me_of(size)
    return [((g // (1 << t)) % 2, (flip(g, 1 << t), c)) for t in range(bits_of(size))]


def targets_of(groups):
    return [target for _, targets in groups for _, target in targets]


def square(x):
    high = x.astype(jnp.bfloat16)
    low = (x - high.astype(jnp.float32)).astype(jnp.bfloat16)

    def dot(p, q):
        return lax.dot_general(
            p, q, (((0,), (0,)), ((), ())), preferred_element_type=jnp.float32
        )

    cross = dot(high, low)
    return dot(high, high) + (cross + cross.T)


def gather_kernel(
    grp, col, b_ref, c_ref, n_ref, b_out, c_out, product_out, third_out, n_out,
    acc, landing, full, *sems,
):
    g, c = me_of(grp)
    rank = b_ref.shape[1]
    groups = [core_group(), chip_group(col), grp_group(grp)]
    others = targets_of(groups[2:])
    greet(targets_of(groups))
    pending = [send(n_ref, n_out, sems[4:], 0, groups[0][1][0][1])]
    for which, (src, out) in enumerate(((c_ref, c_out), (b_ref, b_out))):
        size = src.shape[0]
        mine = out.at[rows_at(g * size, size), :]
        mine[...] = src[...].astype(jnp.bfloat16)
        for number, target in enumerate(others):
            pending.append(send(mine, mine, sems[2:], which * (grp - 1) + number, target))
    for which, src in enumerate((b_ref, c_ref)):
        gram = square(src[...])
        for part in range(rank // LANES):
            first = (which * (rank // LANES) + part) * rank
            acc[first : first + rank, :] = gram[:, part * LANES : (part + 1) * LANES]
    offset, rows = scatter_all(groups, acc, landing, sems)
    full[rows_at(offset, rows), :] = acc[rows_at(offset, rows), :]
    spread_all(groups, full, sems, offset, rows)
    half = acc.shape[0] // 2
    for part in range(rank // LANES):
        second = full[part * rank : (part + 1) * rank, :]
        third = full[half + part * rank : half + (part + 1) * rank, :]
        product_out[:, part * LANES : (part + 1) * LANES] = second * third
        third_out[:, part * LANES : (part + 1) * LANES] = third
    for copy in pending:
        copy.wait()


def first_factor_kernel(
    grp, col, part_ref, inverse_ref, third_ref, update_out, low_out, two_out,
    acc, landing, full, gram, piece, whole, other_inverse, *sems,
):
    g, c = me_of(grp)
    total = part_ref.shape[0]
    own = total // col
    groups = [core_group(), chip_group(col)]
    others = targets_of([grp_group(grp)])
    greet(others + targets_of(groups))
    given = send(inverse_ref, other_inverse, sems[4:], 0, groups[0][1][0][1])
    for block in range(col):
        spot = (block % 2 * (col // 2) + block // 2) * own
        acc[spot : spot + own, :] = part_ref[block * own : (block + 1) * own, :]
    offset, rows = scatter_all(groups, acc, landing, sems)
    given.wait()
    update = jnp.dot(
        acc[rows_at(offset, rows), :],
        inverse_ref[...] + other_inverse[...],
        precision=HIGHEST,
        preferred_element_type=jnp.float32,
    )
    update_out[...] = update
    full[rows_at(offset, rows), :] = update
    spread_all(groups, full, sems, offset, rows)
    gram[...] = square(full[...])
    size = gram.shape[0] // grp
    copies = []
    for number, target in enumerate(others):
        copies.append(
            send(gram.at[rows_at(target[0] * size, size), :], piece.at[number], sems[2:], number, target)
        )
    mine = gram[rows_at(g * size, size), :]
    for number, copy in enumerate(copies):
        copy.wait()
        mine = mine + piece[number]
    spot = whole.at[rows_at(g * size, size), :]
    spot[...] = mine
    copies = [
        send(spot, spot, sems[2:], grp - 1 + number, target) for number, target in enumerate(others)
    ]
    for copy in copies:
        copy.wait()
    gram_first = whole[...]
    row = lax.broadcasted_iota(jnp.int32, gram_first.shape, 0)
    column = lax.broadcasted_iota(jnp.int32, gram_first.shape, 1)
    diagonal = jnp.where(row == column, gram_first, 0.0)
    norm_row = jnp.sqrt(jnp.sum(diagonal, axis=0, keepdims=True) + 1e-06)
    norm_col = jnp.sqrt(jnp.sum(diagonal, axis=1, keepdims=True) + 1e-06)
    two_out[...] = gram_first / (norm_col * norm_row) * third_ref[...]
    for block in range(col):
        first = (block % 2 * (col // 2) + block // 2) * own
        low_out[block * own : (block + 1) * own, :] = (
            full[first : first + own, :] / norm_row
        ).astype(jnp.bfloat16)


def second_factor_kernel(grp, part_ref, inverse_ref, out_ref, other_out, landing, *sems):
    g, c = me_of(grp)
    count = bits_of(grp)
    own = part_ref.shape[0] // grp
    twin = core_group()[1][0][1]
    greet([target for _, target in grp_stages(grp)] + [twin])
    given = send(inverse_ref, other_out, sems[2:], 0, twin)
    half = part_ref.shape[1] // 2
    holding = []
    for h in range(2):
        lanes = slice(h * half, (h + 1) * half)
        holding.append(
            {m: part_ref.at[rows_at(flip(g, m) * own, own), lanes] for m in range(grp)}
        )
    spare = [0, 0]
    used = 0
    for stage in range(count):
        copies = []
        for h in range(2):
            bit = stage if h == 0 else count - 1 - stage
            target = (flip(g, 1 << bit), c)
            for m in sorted(holding[h]):
                if not (m >> bit) & 1:
                    place = landing.at[h, spare[h]]
                    spare[h] += 1
                    source = holding[h][m | (1 << bit)]
                    copies.append((h, m, bit, place, send(source, place, sems, used, target)))
                    used += 1
        for h, m, bit, place, copy in copies:
            copy.wait()
            place[...] += holding[h][m][...]
            holding[h][m] = place
            del holding[h][m | (1 << bit)]
    for h in range(2):
        out_ref[:, h * half : (h + 1) * half] = holding[h][0][...]
    given.wait()


def remote_call(kernel, number, args, outs, scratch):
    vmem = pl.BlockSpec(memory_space=pltpu.VMEM)
    return pl.pallas_call(
        kernel,
        out_shape=[jax.ShapeDtypeStruct(shape, dtype) for shape, dtype in outs],
        in_specs=[vmem] * len(args),
        out_specs=[vmem] * len(outs),
        scratch_shapes=scratch,
        compiler_params=pltpu.CompilerParams(
            collective_id=number, has_side_effects=True, vmem_limit_bytes=VMEM_LIMIT
        ),
    )(*args)


def semaphores(count):
    return [pltpu.SemaphoreType.DMA((count,))] * 2


def on_device(blocks, i_index, j_index, k_index, block_count, b_factor, c_factor):
    edge = blocks.shape[1]
    rank = b_factor.shape[1]
    grp, col = lax.axis_size("grp"), lax.axis_size("col")
    col_links = col // 2
    f32, bf16 = jnp.float32, jnp.bfloat16
    gram_rows = 2 * rank * (rank // LANES)
    b_range, c_range, gram_one, gram_third, twin_count = remote_call(
        functools.partial(gather_kernel, grp, col),
        0,
        (b_factor, c_factor, jnp.broadcast_to(block_count.astype(f32), (8, LANES))),
        [
            ((grp * b_factor.shape[0], rank), bf16),
            ((grp * c_factor.shape[0], rank), bf16),
            ((rank, rank), f32),
            ((rank, rank), f32),
            ((8, LANES), f32),
        ],
        [
            pltpu.VMEM((gram_rows, LANES), f32),
            pltpu.VMEM((gram_rows, LANES), f32),
            pltpu.VMEM((gram_rows, LANES), f32),
        ]
        + semaphores(2 * (col_links + grp - 1))
        + semaphores(2 * (grp - 1))
        + semaphores(1),
    )
    twin = twin_count[0, :1].astype(jnp.int32)
    core = lax.axis_index("col") % 2
    lead = jnp.where(block_count == twin, core == 0, block_count < twin).astype(jnp.int32)
    scalars = (i_index, j_index, k_index, block_count)
    own_rows = 2 * edge
    first_rows = own_rows * col
    partial_one = mode_call(mode_one_kernel, scalars, blocks, b_range, c_range, first_rows, [])
    a_update, a_range, gram_two = remote_call(
        functools.partial(first_factor_kernel, grp, col),
        1,
        (partial_one, inverse(lead, gram_one), gram_third),
        [((own_rows, rank), f32), ((first_rows, rank), bf16), ((rank, rank), f32)],
        [
            pltpu.VMEM((first_rows, rank), f32),
            pltpu.VMEM((first_rows, rank), f32),
            pltpu.VMEM((first_rows, rank), f32),
            pltpu.VMEM((rank, rank), f32),
            pltpu.VMEM((grp - 1, rank // grp, rank), f32),
            pltpu.VMEM((rank, rank), f32),
            pltpu.VMEM((rank, rank), f32),
        ]
        + semaphores(2 * col_links)
        + semaphores(2 * (grp - 1))
        + semaphores(1),
    )
    inverse_two = inverse(lead, gram_two)
    second_rows = b_range.shape[0]
    partial_two = mode_call(
        mode_two_kernel,
        scalars,
        blocks,
        a_range,
        c_range,
        second_rows,
        [pltpu.VMEM((UNROLL, 8 * edge, LANES), f32)],
    )
    own_sum, twin_inverse = remote_call(
        functools.partial(second_factor_kernel, grp),
        2,
        (partial_two, inverse_two),
        [((second_rows // grp, rank), f32), ((rank, rank), f32)],
        [pltpu.VMEM((2, grp - 1, second_rows // grp, rank // 2), f32)]
        + semaphores(2 * (grp - 1))
        + semaphores(1),
    )
    b_update = pl.pallas_call(
        solve_kernel,
        out_shape=jax.ShapeDtypeStruct(own_sum.shape, f32),
        in_specs=[pl.BlockSpec(memory_space=pltpu.VMEM)] * 3,
        out_specs=pl.BlockSpec(memory_space=pltpu.VMEM),
        compiler_params=pltpu.CompilerParams(vmem_limit_bytes=VMEM_LIMIT),
    )(own_sum, inverse_two, twin_inverse)
    return (a_update, b_update)


def solution(mesh):
    return jax.shard_map(
        on_device,
        mesh=mesh,
        in_specs=(
            P(("grp", "col"), None, None),
            P(("grp", "col")),
            P(("grp", "col")),
            P(("grp", "col")),
            P(("grp", "col")),
            P(("grp", "col"), None),
            P(("grp", "col"), None),
        ),
        out_specs=(P(("grp", "col"), None), P(("grp", "col"), None)),
        check_vma=False,
    )
```

```python
import functools
import jax
import jax.numpy as jnp
from jax import lax
from jax.experimental import pallas as pl
from jax.experimental.pallas import tpu as pltpu
from jax.sharding import PartitionSpec as P

HIGHEST = lax.Precision.HIGHEST
GROUP = 32
UNROLL = 16
QUARTER = 32
LANES = 128
VMEM_LIMIT = 56 * 1024 * 1024


def khatri_rao(left, tail, first):
    rows = [
        jnp.broadcast_to(left[first + t : first + t + 1, :], tail.shape).astype(jnp.bfloat16) * tail
        for t in range(8)
    ]
    return jnp.concatenate(rows, axis=0)


def product_rows(lhs_part, left, tail):
    total = None
    for q in range(4):
        term = jnp.dot(
            lhs_part(q), khatri_rao(left, tail, 8 * q), preferred_element_type=jnp.float32
        )
        total = term if total is None else total + term
    return total


def slot_loop(count, do_slot):
    base = pl.program_id(0) * GROUP
    steps = jnp.clip((count - base + UNROLL - 1) // UNROLL, 0, GROUP // UNROLL)

    def body(step, carry):
        for u in range(UNROLL):
            local = step * UNROLL + u
            do_slot(local, base + local, u)
        return carry

    lax.fori_loop(0, steps, body, 0)


def mode_one_kernel(i_ref, j_ref, k_ref, n_ref, x_ref, b_ref, c_ref, out_ref):
    @pl.when(pl.program_id(0) == 0)
    def _():
        out_ref[...] = jnp.zeros_like(out_ref)

    count = n_ref[0]

    def do_slot(local, slot, u):
        left = b_ref[pl.ds(pl.multiple_of(j_ref[slot] * 32, 32), 32), :].astype(jnp.float32)
        tail = c_ref[pl.ds(pl.multiple_of(k_ref[slot] * 32, 32), 32), :]
        result = product_rows(lambda q: x_ref[local, :, q * 256 : (q + 1) * 256], left, tail)
        alive = (slot < count).astype(jnp.float32)
        rows = pl.ds(pl.multiple_of(i_ref[slot] * 32, 32), 32)
        out_ref[rows, :] += result * alive

    slot_loop(count, do_slot)


def quarter_swap(parts):
    lane = lax.broadcasted_iota(jnp.int32, parts[0].shape, 1)
    even = (lane // QUARTER) % 2 == 0
    low = lane < 2 * QUARTER

    def pair(p, q, keep, dist):
        return (
            jnp.where(keep, p, pltpu.roll(q, dist, 1)),
            jnp.where(keep, pltpu.roll(p, LANES - dist, 1), q),
        )

    p0, p1 = pair(parts[0], parts[1], even, QUARTER)
    p2, p3 = pair(parts[2], parts[3], even, QUARTER)
    r0, r2 = pair(p0, p2, low, 2 * QUARTER)
    r1, r3 = pair(p1, p3, low, 2 * QUARTER)
    return [r0, r1, r2, r3]


def mode_two_kernel(i_ref, j_ref, k_ref, n_ref, x_ref, a_ref, c_ref, out_ref, wide):
    @pl.when(pl.program_id(0) == 0)
    def _():
        out_ref[...] = jnp.zeros_like(out_ref)

    count = n_ref[0]

    def do_slot(local, slot, u):
        for col in range(8):
            wide[u, 32 * col : 32 * col + 32, :] = x_ref[
                local, :, col * LANES : (col + 1) * LANES
            ].astype(jnp.float32)

        def lhs_part(q):
            pieces = []
            for half in range(2):
                first = q * 8 + half * 4
                parts = [wide[u, pl.ds(first + t, 8, stride=32), :] for t in range(4)]
                pieces.append(jnp.concatenate(quarter_swap(parts), axis=0).astype(jnp.bfloat16))
            return jnp.concatenate(pieces, axis=1)

        left = a_ref[pl.ds(pl.multiple_of(i_ref[slot] * 32, 32), 32), :].astype(jnp.float32)
        tail = c_ref[pl.ds(pl.multiple_of(k_ref[slot] * 32, 32), 32), :]
        result = product_rows(lhs_part, left, tail)
        alive = (slot < count).astype(jnp.float32)
        rows = pl.ds(pl.multiple_of(j_ref[slot] * 32, 32), 32)
        out_ref[rows, :] += result * alive

    slot_loop(count, do_slot)


def mode_call(kernel, scalars, blocks, left, tail, rows, scratch):
    slots, edge, width = blocks.shape
    rank = left.shape[1]
    grid_spec = pltpu.PrefetchScalarGridSpec(
        num_scalar_prefetch=4,
        grid=(slots // GROUP,),
        in_specs=[
            pl.BlockSpec((GROUP, edge, width), lambda g, *_: (g, 0, 0)),
            pl.BlockSpec(left.shape, lambda g, *_: (0, 0)),
            pl.BlockSpec(tail.shape, lambda g, *_: (0, 0)),
        ],
        out_specs=pl.BlockSpec((rows, rank), lambda g, *_: (0, 0)),
        scratch_shapes=scratch,
    )
    return pl.pallas_call(
        kernel,
        grid_spec=grid_spec,
        out_shape=jax.ShapeDtypeStruct((rows, rank), jnp.float32),
        compiler_params=pltpu.CompilerParams(vmem_limit_bytes=VMEM_LIMIT),
        cost_estimate=pl.CostEstimate(
            flops=2 * slots * edge * width * rank,
            bytes_accessed=2 * slots * edge * width,
            transcendentals=0,
        ),
    )(*scalars, blocks, left, tail)


def inverse_kernel(lead_ref, g_ref, out_ref):
    @pl.when(lead_ref[0] == 0)
    def _():
        out_ref[...] = jnp.zeros_like(out_ref)

    @pl.when(lead_ref[0] != 0)
    def _():
        out_ref[...] = newton_inverse(g_ref[...])


def newton_inverse(gram):
    row = lax.broadcasted_iota(jnp.int32, gram.shape, 0)
    col = lax.broadcasted_iota(jnp.int32, gram.shape, 1)
    eye = (row == col).astype(jnp.float32)
    scale_row = lax.rsqrt(jnp.sum(gram * eye, axis=0, keepdims=True))
    scale_col = lax.rsqrt(jnp.sum(gram * eye, axis=1, keepdims=True))
    unit = gram * scale_row * scale_col
    bound = 1.0 / jnp.max(jnp.sum(jnp.abs(unit), axis=0, keepdims=True))

    def residual(x):
        return eye - jnp.dot(unit, x, precision=HIGHEST, preferred_element_type=jnp.float32)

    def update(x, r):
        return x + jnp.dot(x, r, precision=HIGHEST, preferred_element_type=jnp.float32)

    unit_low = unit.astype(jnp.bfloat16)

    def body_low(state):
        step, _, x, r = state
        x = x + jnp.dot(
            x.astype(jnp.bfloat16), r.astype(jnp.bfloat16), preferred_element_type=jnp.float32
        )
        r = eye - jnp.dot(unit_low, x.astype(jnp.bfloat16), preferred_element_type=jnp.float32)
        return step + 1, jnp.sum(r * r), x, r

    def body(state):
        step, _, x, r = state
        x = update(x, r)
        r = residual(x)
        return step + 1, jnp.sum(r * r), x, r

    def more_low(state):
        return jnp.logical_and(state[0] < 16, state[1] > 0.01)

    def more(state):
        return jnp.logical_and(state[0] < 60, state[1] > 1e-6)

    start = eye * bound
    start_r = eye - unit * bound
    _, _, x, _ = lax.while_loop(
        more_low, body_low, (jnp.int32(0), jnp.sum(start_r * start_r), start, start_r)
    )
    r = residual(x)
    good = jnp.sum(r * r) < 0.25
    x = jnp.where(good, x, start)
    r = jnp.where(good, r, start_r)
    _, _, x, r = lax.while_loop(more, body, (jnp.int32(0), jnp.sum(r * r), x, r))
    return update(x, r) * scale_row * scale_col


def inverse(lead, gram):
    return pl.pallas_call(
        inverse_kernel,
        out_shape=jax.ShapeDtypeStruct(gram.shape, jnp.float32),
        in_specs=[
            pl.BlockSpec(memory_space=pltpu.SMEM),
            pl.BlockSpec(memory_space=pltpu.VMEM),
        ],
        out_specs=pl.BlockSpec(memory_space=pltpu.VMEM),
        compiler_params=pltpu.CompilerParams(vmem_limit_bytes=VMEM_LIMIT),
    )(lead, gram)


def solve_kernel(sum_ref, mine_ref, other_ref, out_ref):
    own, rank = sum_ref.shape
    solved = jnp.dot(
        sum_ref[...],
        mine_ref[...] + other_ref[...],
        precision=HIGHEST,
        preferred_element_type=jnp.float32,
    )
    out_ref[...] = solved.reshape(own // 32, 4, 8, rank).swapaxes(1, 2).reshape(own, rank)


def me_of(shape):
    return lax.axis_index("grp"), lax.axis_index("col")


def bits_of(size):
    count = size.bit_length() - 1
    assert size == 1 << count
    return count


def flip(position, mask):
    out = position
    for t in range(mask.bit_length()):
        if (mask >> t) & 1:
            bit = (position // (1 << t)) % 2
            out = out + (1 - 2 * bit) * (1 << t)
    return out


def greet(targets):
    barrier = pltpu.get_barrier_semaphore()
    for target in targets:
        pl.semaphore_signal(barrier, inc=1, device_id=target, device_id_type=pl.DeviceIdType.MESH)
    pl.semaphore_wait(barrier, len(targets))


def send(src, dst, sems, index, target):
    copy = pltpu.make_async_remote_copy(
        src_ref=src,
        dst_ref=dst,
        send_sem=sems[0].at[index],
        recv_sem=sems[1].at[index],
        device_id=target,
        device_id_type=pl.DeviceIdType.MESH,
    )
    copy.start()
    return copy


def rows_at(first, size):
    return pl.ds(pl.multiple_of(first, 8), size)


def scatter_sum(group, acc, landing, sems, first, offset, rows):
    index, targets = group
    size = len(targets) + 1
    chunk = rows // size
    copies = []
    for number, (other, target) in enumerate(targets):
        place = landing.at[pl.ds(rows - (number + 1) * chunk, chunk), :]
        copies.append(
            send(acc.at[rows_at(offset + other * chunk, chunk), :], place, sems, first + number, target)
        )
    offset = offset + index * chunk
    for number, copy in enumerate(copies):
        copy.wait()
        low = rows - (number + 1) * chunk
        acc[rows_at(offset, chunk), :] += landing[low : low + chunk, :]
    return offset, chunk


def spread(group, full, sems, first, offset, rows):
    index, targets = group
    copies = []
    mine = full.at[rows_at(offset, rows), :]
    for number, (_, target) in enumerate(targets):
        copies.append(send(mine, mine, sems, first + number, target))
    for copy in copies:
        copy.wait()
    return offset - index * rows, rows * (len(targets) + 1)


def scatter_all(groups, acc, landing, sems):
    offset, rows, first = jnp.int32(0), acc.shape[0], 0
    for group in groups:
        offset, rows = scatter_sum(group, acc, landing, sems, first, offset, rows)
        first += len(group[1])
    return offset, rows


def spread_all(groups, full, sems, offset, rows):
    first = sum(len(group[1]) for group in groups)
    for group in reversed(groups):
        offset, rows = spread(group, full, sems, first, offset, rows)
        first += len(group[1])


def core_group():
    g, c = lax.axis_index("grp"), lax.axis_index("col")
    core = lax.rem(c, 2)
    return core, [(1 - core, (g, c + 1 - 2 * core))]


def chip_group(col):
    g, c = lax.axis_index("grp"), lax.axis_index("col")
    chips, core, chip = col // 2, lax.rem(c, 2), c // 2
    others = [lax.rem(chip + p, chips) for p in range(1, chips)]
    return chip, [(other, (g, other * 2 + core)) for other in others]


def grp_group(grp):
    g, c = lax.axis_index("grp"), lax.axis_index("col")
    others = [lax.rem(g + p, grp) for p in range(1, grp)]
    return g, [(other, (other, c)) for other in others]


def grp_stages(size):
    g, c = me_of(size)
    return [((g // (1 << t)) % 2, (flip(g, 1 << t), c)) for t in range(bits_of(size))]


def targets_of(groups):
    return [target for _, targets in groups for _, target in targets]


def square(x):
    high = x.astype(jnp.bfloat16)
    low = (x - high.astype(jnp.float32)).astype(jnp.bfloat16)

    def dot(p, q):
        return lax.dot_general(
            p, q, (((0,), (0,)), ((), ())), preferred_element_type=jnp.float32
        )

    cross = dot(high, low)
    return dot(high, high) + (cross + cross.T)


def gram_blocks(rank, grams, devices):
    side = rank // LANES
    upper = [(w, r, c) for w in range(grams) for r in range(side) for c in range(r, side)]
    if len(upper) * LANES % (8 * devices) == 0:
        return upper
    return [(w, r, c) for w in range(grams) for r in range(side) for c in range(side)]


def pack_gram(blocks, which, gram, ref):
    for number, (w, r, c) in enumerate(blocks):
        if w == which:
            ref[number * LANES : (number + 1) * LANES, :] = gram[
                r * LANES : (r + 1) * LANES, c * LANES : (c + 1) * LANES
            ]


def unpack_gram(blocks, which, ref):
    found = {}
    for number, (w, r, c) in enumerate(blocks):
        if w == which:
            found[r, c] = ref[number * LANES : (number + 1) * LANES, :]
    for r, c in list(found):
        if (c, r) not in found:
            found[c, r] = found[r, c].T
    side = max(r for r, _ in found) + 1
    return jnp.concatenate(
        [jnp.concatenate([found[r, c] for c in range(side)], axis=1) for r in range(side)], axis=0
    )


def gather_kernel(
    grp, col, b_ref, c_ref, n_ref, b_out, c_out, product_out, third_out, n_out,
    acc, landing, full, *sems,
):
    g, c = me_of(grp)
    rank = b_ref.shape[1]
    groups = [core_group(), chip_group(col), grp_group(grp)]
    others = targets_of(groups[2:])
    greet(targets_of(groups))
    pending = [send(n_ref, n_out, sems[4:], 0, groups[0][1][0][1])]
    for which, (src, out) in enumerate(((c_ref, c_out), (b_ref, b_out))):
        size = src.shape[0]
        mine = out.at[rows_at(g * size, size), :]
        mine[...] = src[...].astype(jnp.bfloat16)
        for number, target in enumerate(others):
            pending.append(send(mine, mine, sems[2:], which * (grp - 1) + number, target))
    layout = gram_blocks(rank, 2, grp * col)
    pack_gram(layout, 0, square(b_ref[...]), acc)
    pack_gram(layout, 1, square(c_ref[...]), acc)
    offset, rows = scatter_all(groups, acc, landing, sems)
    full[rows_at(offset, rows), :] = acc[rows_at(offset, rows), :]
    spread_all(groups, full, sems, offset, rows)
    third = unpack_gram(layout, 1, full)
    product_out[...] = unpack_gram(layout, 0, full) * third
    third_out[...] = third
    for copy in pending:
        copy.wait()


def first_factor_kernel(
    grp, col, part_ref, inverse_ref, third_ref, update_out, low_out, two_out,
    acc, landing, full, gram, piece, whole, other_inverse, *sems,
):
    g, c = me_of(grp)
    total, gram_rank = part_ref.shape
    own = total // col
    groups = [core_group(), chip_group(col)]
    others = targets_of([grp_group(grp)])
    greet(others + targets_of(groups))
    given = send(inverse_ref, other_inverse, sems[4:], 0, groups[0][1][0][1])
    for block in range(col):
        spot = (block % 2 * (col // 2) + block // 2) * own
        acc[spot : spot + own, :] = part_ref[block * own : (block + 1) * own, :]
    offset, rows = scatter_all(groups, acc, landing, sems)
    given.wait()
    update = jnp.dot(
        acc[rows_at(offset, rows), :],
        inverse_ref[...] + other_inverse[...],
        precision=HIGHEST,
        preferred_element_type=jnp.float32,
    )
    update_out[...] = update
    full[rows_at(offset, rows), :] = update
    spread_all(groups, full, sems, offset, rows)
    layout = gram_blocks(gram_rank, 1, grp)
    pack_gram(layout, 0, square(full[...]), gram)
    groups = [grp_group(grp)]
    offset, rows = scatter_all(groups, gram, piece, sems[2:])
    whole[rows_at(offset, rows), :] = gram[rows_at(offset, rows), :]
    spread_all(groups, whole, sems[2:], offset, rows)
    gram_first = unpack_gram(layout, 0, whole)
    row = lax.broadcasted_iota(jnp.int32, gram_first.shape, 0)
    column = lax.broadcasted_iota(jnp.int32, gram_first.shape, 1)
    diagonal = jnp.where(row == column, gram_first, 0.0)
    norm_row = jnp.sqrt(jnp.sum(diagonal, axis=0, keepdims=True) + 1e-06)
    norm_col = jnp.sqrt(jnp.sum(diagonal, axis=1, keepdims=True) + 1e-06)
    two_out[...] = gram_first / (norm_col * norm_row) * third_ref[...]
    for block in range(col):
        first = (block % 2 * (col // 2) + block // 2) * own
        low_out[block * own : (block + 1) * own, :] = (
            full[first : first + own, :] / norm_row
        ).astype(jnp.bfloat16)


def second_factor_kernel(grp, part_ref, out_ref, landing, *sems):
    g, c = me_of(grp)
    count = bits_of(grp)
    own = part_ref.shape[0] // grp
    greet([target for _, target in grp_stages(grp)])
    half = part_ref.shape[1] // 2
    holding = []
    for h in range(2):
        lanes = slice(h * half, (h + 1) * half)
        holding.append(
            {m: part_ref.at[rows_at(flip(g, m) * own, own), lanes] for m in range(grp)}
        )
    spare = [0, 0]
    used = 0
    for stage in range(count):
        copies = []
        for h in range(2):
            bit = stage if h == 0 else count - 1 - stage
            target = (flip(g, 1 << bit), c)
            for m in sorted(holding[h]):
                if not (m >> bit) & 1:
                    place = landing.at[h, spare[h]]
                    spare[h] += 1
                    source = holding[h][m | (1 << bit)]
                    copies.append((h, m, bit, place, send(source, place, sems, used, target)))
                    used += 1
        for h, m, bit, place, copy in copies:
            copy.wait()
            place[...] += holding[h][m][...]
            holding[h][m] = place
            del holding[h][m | (1 << bit)]
    for h in range(2):
        out_ref[:, h * half : (h + 1) * half] = holding[h][0][...]


def remote_call(kernel, number, args, outs, scratch):
    vmem = pl.BlockSpec(memory_space=pltpu.VMEM)
    return pl.pallas_call(
        kernel,
        out_shape=[jax.ShapeDtypeStruct(shape, dtype) for shape, dtype in outs],
        in_specs=[vmem] * len(args),
        out_specs=[vmem] * len(outs),
        scratch_shapes=scratch,
        compiler_params=pltpu.CompilerParams(
            collective_id=number, has_side_effects=True, vmem_limit_bytes=VMEM_LIMIT
        ),
    )(*args)


def semaphores(count):
    return [pltpu.SemaphoreType.DMA((count,))] * 2


def on_device(blocks, i_index, j_index, k_index, block_count, b_factor, c_factor):
    edge = blocks.shape[1]
    rank = b_factor.shape[1]
    grp, col = lax.axis_size("grp"), lax.axis_size("col")
    col_links = col // 2
    f32, bf16 = jnp.float32, jnp.bfloat16
    gram_rows = len(gram_blocks(rank, 2, grp * col)) * LANES
    first_gram = len(gram_blocks(rank, 1, grp)) * LANES
    b_range, c_range, gram_one, gram_third, twin_count = remote_call(
        functools.partial(gather_kernel, grp, col),
        0,
        (b_factor, c_factor, jnp.broadcast_to(block_count.astype(f32), (8, LANES))),
        [
            ((grp * b_factor.shape[0], rank), bf16),
            ((grp * c_factor.shape[0], rank), bf16),
            ((rank, rank), f32),
            ((rank, rank), f32),
            ((8, LANES), f32),
        ],
        [
            pltpu.VMEM((gram_rows, LANES), f32),
            pltpu.VMEM((gram_rows, LANES), f32),
            pltpu.VMEM((gram_rows, LANES), f32),
        ]
        + semaphores(2 * (col_links + grp - 1))
        + semaphores(2 * (grp - 1))
        + semaphores(1),
    )
    twin = twin_count[0, :1].astype(jnp.int32)
    core = lax.axis_index("col") % 2
    lead = jnp.where(block_count == twin, core == 0, block_count < twin).astype(jnp.int32)
    scalars = (i_index, j_index, k_index, block_count)
    own_rows = 2 * edge
    first_rows = own_rows * col
    partial_one = mode_call(mode_one_kernel, scalars, blocks, b_range, c_range, first_rows, [])
    a_update, a_range, gram_two = remote_call(
        functools.partial(first_factor_kernel, grp, col),
        1,
        (partial_one, inverse(lead, gram_one), gram_third),
        [((own_rows, rank), f32), ((first_rows, rank), bf16), ((rank, rank), f32)],
        [
            pltpu.VMEM((first_rows, rank), f32),
            pltpu.VMEM((first_rows, rank), f32),
            pltpu.VMEM((first_rows, rank), f32),
            pltpu.VMEM((first_gram, LANES), f32),
            pltpu.VMEM((first_gram, LANES), f32),
            pltpu.VMEM((first_gram, LANES), f32),
            pltpu.VMEM((rank, rank), f32),
        ]
        + semaphores(2 * col_links)
        + semaphores(2 * (grp - 1))
        + semaphores(1),
    )
    inverse_two = inverse(lead, gram_two)
    twin_inverse = lax.ppermute(
        inverse_two, "col", [(c, c + 1 - 2 * (c % 2)) for c in range(col)]
    )
    second_rows = b_range.shape[0]
    partial_two = mode_call(
        mode_two_kernel,
        scalars,
        blocks,
        a_range,
        c_range,
        second_rows,
        [pltpu.VMEM((UNROLL, 8 * edge, LANES), f32)],
    )
    (own_sum,) = remote_call(
        functools.partial(second_factor_kernel, grp),
        2,
        (partial_two,),
        [((second_rows // grp, rank), f32)],
        [pltpu.VMEM((2, grp - 1, second_rows // grp, rank // 2), f32)]
        + semaphores(2 * (grp - 1)),
    )
    b_update = pl.pallas_call(
        solve_kernel,
        out_shape=jax.ShapeDtypeStruct(own_sum.shape, f32),
        in_specs=[pl.BlockSpec(memory_space=pltpu.VMEM)] * 3,
        out_specs=pl.BlockSpec(memory_space=pltpu.VMEM),
        compiler_params=pltpu.CompilerParams(vmem_limit_bytes=VMEM_LIMIT),
    )(own_sum, inverse_two, twin_inverse)
    return (a_update, b_update)


def solution(mesh):
    return jax.shard_map(
        on_device,
        mesh=mesh,
        in_specs=(
            P(("grp", "col"), None, None),
            P(("grp", "col")),
            P(("grp", "col")),
            P(("grp", "col")),
            P(("grp", "col")),
            P(("grp", "col"), None),
            P(("grp", "col"), None),
        ),
        out_specs=(P(("grp", "col"), None), P(("grp", "col"), None)),
        check_vma=False,
    )
```

```python
import functools
import jax
import jax.numpy as jnp
from jax import lax
from jax.experimental import pallas as pl
from jax.experimental.pallas import tpu as pltpu
from jax.sharding import PartitionSpec as P

HIGHEST = lax.Precision.HIGHEST
GROUP = 32
UNROLL = 32
WARM_STEPS = 10
QUARTER = 32
LANES = 128
VMEM_LIMIT = 56 * 1024 * 1024


def khatri_rao(left, tail, first):
    rows = [
        jnp.broadcast_to(left[first + t : first + t + 1, :], tail.shape).astype(jnp.bfloat16) * tail
        for t in range(8)
    ]
    return jnp.concatenate(rows, axis=0)


def product_rows(lhs_part, left, tail):
    total = None
    for q in range(4):
        term = jnp.dot(
            lhs_part(q), khatri_rao(left, tail, 8 * q), preferred_element_type=jnp.float32
        )
        total = term if total is None else total + term
    return total


def slot_loop(count, do_slot):
    base = pl.program_id(0) * GROUP
    steps = jnp.clip((count - base + UNROLL - 1) // UNROLL, 0, GROUP // UNROLL)

    def body(step, carry):
        for u in range(UNROLL):
            local = step * UNROLL + u
            do_slot(local, base + local, u)
        return carry

    lax.fori_loop(0, steps, body, 0)


def mode_one_kernel(i_ref, j_ref, k_ref, n_ref, x_ref, b_ref, c_ref, out_ref):
    @pl.when(pl.program_id(0) == 0)
    def _():
        out_ref[...] = jnp.zeros_like(out_ref)

    count = n_ref[0]

    def do_slot(local, slot, u):
        left = b_ref[pl.ds(pl.multiple_of(j_ref[slot] * 32, 32), 32), :].astype(jnp.float32)
        tail = c_ref[pl.ds(pl.multiple_of(k_ref[slot] * 32, 32), 32), :]
        result = product_rows(lambda q: x_ref[local, :, q * 256 : (q + 1) * 256], left, tail)
        alive = (slot < count).astype(jnp.float32)
        rows = pl.ds(pl.multiple_of(i_ref[slot] * 32, 32), 32)
        out_ref[rows, :] += result * alive

    slot_loop(count, do_slot)


def quarter_swap(parts):
    lane = lax.broadcasted_iota(jnp.int32, parts[0].shape, 1)
    even = (lane // QUARTER) % 2 == 0
    low = lane < 2 * QUARTER

    def pair(p, q, keep, dist):
        return (
            jnp.where(keep, p, pltpu.roll(q, dist, 1)),
            jnp.where(keep, pltpu.roll(p, LANES - dist, 1), q),
        )

    p0, p1 = pair(parts[0], parts[1], even, QUARTER)
    p2, p3 = pair(parts[2], parts[3], even, QUARTER)
    r0, r2 = pair(p0, p2, low, 2 * QUARTER)
    r1, r3 = pair(p1, p3, low, 2 * QUARTER)
    return [r0, r1, r2, r3]


def mode_two_kernel(i_ref, j_ref, k_ref, n_ref, x_ref, a_ref, c_ref, out_ref, wide):
    @pl.when(pl.program_id(0) == 0)
    def _():
        out_ref[...] = jnp.zeros_like(out_ref)

    count = n_ref[0]

    def do_slot(local, slot, u):
        for col in range(8):
            wide[u, 32 * col : 32 * col + 32, :] = x_ref[
                local, :, col * LANES : (col + 1) * LANES
            ].astype(jnp.float32)

        def lhs_part(q):
            pieces = []
            for half in range(2):
                first = q * 8 + half * 4
                parts = [wide[u, pl.ds(first + t, 8, stride=32), :] for t in range(4)]
                pieces.append(jnp.concatenate(quarter_swap(parts), axis=0).astype(jnp.bfloat16))
            return jnp.concatenate(pieces, axis=1)

        left = a_ref[pl.ds(pl.multiple_of(i_ref[slot] * 32, 32), 32), :].astype(jnp.float32)
        tail = c_ref[pl.ds(pl.multiple_of(k_ref[slot] * 32, 32), 32), :]
        result = product_rows(lhs_part, left, tail)
        alive = (slot < count).astype(jnp.float32)
        rows = pl.ds(pl.multiple_of(j_ref[slot] * 32, 32), 32)
        out_ref[rows, :] += result * alive

    slot_loop(count, do_slot)


def mode_call(kernel, scalars, blocks, left, tail, rows, scratch):
    slots, edge, width = blocks.shape
    rank = left.shape[1]
    grid_spec = pltpu.PrefetchScalarGridSpec(
        num_scalar_prefetch=4,
        grid=(slots // GROUP,),
        in_specs=[
            pl.BlockSpec((GROUP, edge, width), lambda g, *_: (g, 0, 0)),
            pl.BlockSpec(left.shape, lambda g, *_: (0, 0)),
            pl.BlockSpec(tail.shape, lambda g, *_: (0, 0)),
        ],
        out_specs=pl.BlockSpec((rows, rank), lambda g, *_: (0, 0)),
        scratch_shapes=scratch,
    )
    return pl.pallas_call(
        kernel,
        grid_spec=grid_spec,
        out_shape=jax.ShapeDtypeStruct((rows, rank), jnp.float32),
        compiler_params=pltpu.CompilerParams(vmem_limit_bytes=VMEM_LIMIT),
        cost_estimate=pl.CostEstimate(
            flops=2 * slots * edge * width * rank,
            bytes_accessed=2 * slots * edge * width,
            transcendentals=0,
        ),
    )(*scalars, blocks, left, tail)


def inverse_kernel(lead_ref, g_ref, out_ref):
    @pl.when(lead_ref[0] == 0)
    def _():
        out_ref[...] = jnp.zeros_like(out_ref)

    @pl.when(lead_ref[0] != 0)
    def _():
        out_ref[...] = newton_inverse(g_ref[...])


def scaled_gram(gram):
    row = lax.broadcasted_iota(jnp.int32, gram.shape, 0)
    col = lax.broadcasted_iota(jnp.int32, gram.shape, 1)
    eye = (row == col).astype(jnp.float32)
    scale_row = lax.rsqrt(jnp.sum(gram * eye, axis=0, keepdims=True))
    scale_col = lax.rsqrt(jnp.sum(gram * eye, axis=1, keepdims=True))
    unit = gram * scale_row * scale_col
    bound = 1.0 / jnp.max(jnp.sum(jnp.abs(unit), axis=0, keepdims=True))
    return eye, unit, scale_row, scale_col, eye * bound, eye - unit * bound


def low_step(eye, unit_low, x, r):
    x = x + jnp.dot(
        x.astype(jnp.bfloat16), r.astype(jnp.bfloat16), preferred_element_type=jnp.float32
    )
    r = eye - jnp.dot(unit_low, x.astype(jnp.bfloat16), preferred_element_type=jnp.float32)
    return x, r


def finish_inverse(scaled, x):
    eye, unit, scale_row, scale_col, start, start_r = scaled

    def residual(x):
        return eye - jnp.dot(unit, x, precision=HIGHEST, preferred_element_type=jnp.float32)

    def update(x, r):
        return x + jnp.dot(x, r, precision=HIGHEST, preferred_element_type=jnp.float32)

    def body(state):
        step, _, x, r = state
        x = update(x, r)
        r = residual(x)
        return step + 1, jnp.sum(r * r), x, r

    def more(state):
        return jnp.logical_and(state[0] < 60, state[1] > 1e-6)

    r = residual(x)
    good = jnp.sum(r * r) < 0.25
    x = jnp.where(good, x, start)
    r = jnp.where(good, r, start_r)
    _, _, x, r = lax.while_loop(more, body, (jnp.int32(0), jnp.sum(r * r), x, r))
    return update(x, r) * scale_row * scale_col


def newton_inverse(gram):
    scaled = scaled_gram(gram)
    eye, unit, _, _, start, start_r = scaled
    unit_low = unit.astype(jnp.bfloat16)

    def body_low(state):
        step, _, x, r = state
        x, r = low_step(eye, unit_low, x, r)
        return step + 1, jnp.sum(r * r), x, r

    def more_low(state):
        return jnp.logical_and(state[0] < 16, state[1] > 0.01)

    _, _, x, _ = lax.while_loop(
        more_low, body_low, (jnp.int32(0), jnp.sum(start_r * start_r), start, start_r)
    )
    return finish_inverse(scaled, x)


def inverse(lead, gram):
    return pl.pallas_call(
        inverse_kernel,
        out_shape=jax.ShapeDtypeStruct(gram.shape, jnp.float32),
        in_specs=[
            pl.BlockSpec(memory_space=pltpu.SMEM),
            pl.BlockSpec(memory_space=pltpu.VMEM),
        ],
        out_specs=pl.BlockSpec(memory_space=pltpu.VMEM),
        compiler_params=pltpu.CompilerParams(vmem_limit_bytes=VMEM_LIMIT),
    )(lead, gram)


def solve_kernel(sum_ref, gram_ref, warm_ref, out_ref):
    own, rank = sum_ref.shape
    solved = jnp.dot(
        sum_ref[...],
        finish_inverse(scaled_gram(gram_ref[...]), warm_ref[...]),
        precision=HIGHEST,
        preferred_element_type=jnp.float32,
    )
    out_ref[...] = solved.reshape(own // 32, 4, 8, rank).swapaxes(1, 2).reshape(own, rank)


def me_of(shape):
    return lax.axis_index("grp"), lax.axis_index("col")


def bits_of(size):
    count = size.bit_length() - 1
    assert size == 1 << count
    return count


def flip(position, mask):
    out = position
    for t in range(mask.bit_length()):
        if (mask >> t) & 1:
            bit = (position // (1 << t)) % 2
            out = out + (1 - 2 * bit) * (1 << t)
    return out


def greet(targets):
    barrier = pltpu.get_barrier_semaphore()
    for target in targets:
        pl.semaphore_signal(barrier, inc=1, device_id=target, device_id_type=pl.DeviceIdType.MESH)
    pl.semaphore_wait(barrier, len(targets))


def send(src, dst, sems, index, target):
    copy = pltpu.make_async_remote_copy(
        src_ref=src,
        dst_ref=dst,
        send_sem=sems[0].at[index],
        recv_sem=sems[1].at[index],
        device_id=target,
        device_id_type=pl.DeviceIdType.MESH,
    )
    copy.start()
    return copy


def rows_at(first, size):
    return pl.ds(pl.multiple_of(first, 8), size)


def scatter_sum(group, acc, landing, sems, first, offset, rows):
    index, targets = group
    size = len(targets) + 1
    chunk = rows // size
    copies = []
    for number, (other, target) in enumerate(targets):
        place = landing.at[pl.ds(rows - (number + 1) * chunk, chunk), :]
        copies.append(
            send(acc.at[rows_at(offset + other * chunk, chunk), :], place, sems, first + number, target)
        )
    offset = offset + index * chunk
    for number, copy in enumerate(copies):
        copy.wait()
        low = rows - (number + 1) * chunk
        acc[rows_at(offset, chunk), :] += landing[low : low + chunk, :]
    return offset, chunk


def spread(group, full, sems, first, offset, rows):
    index, targets = group
    copies = []
    mine = full.at[rows_at(offset, rows), :]
    for number, (_, target) in enumerate(targets):
        copies.append(send(mine, mine, sems, first + number, target))
    for copy in copies:
        copy.wait()
    return offset - index * rows, rows * (len(targets) + 1)


def scatter_all(groups, acc, landing, sems):
    offset, rows, first = jnp.int32(0), acc.shape[0], 0
    for group in groups:
        offset, rows = scatter_sum(group, acc, landing, sems, first, offset, rows)
        first += len(group[1])
    return offset, rows


def spread_all(groups, full, sems, offset, rows):
    first = sum(len(group[1]) for group in groups)
    for group in reversed(groups):
        offset, rows = spread(group, full, sems, first, offset, rows)
        first += len(group[1])


def core_group():
    g, c = lax.axis_index("grp"), lax.axis_index("col")
    core = lax.rem(c, 2)
    return core, [(1 - core, (g, c + 1 - 2 * core))]


def chip_group(col):
    g, c = lax.axis_index("grp"), lax.axis_index("col")
    chips, core, chip = col // 2, lax.rem(c, 2), c // 2
    others = [lax.rem(chip + p, chips) for p in range(1, chips)]
    return chip, [(other, (g, other * 2 + core)) for other in others]


def grp_group(grp):
    g, c = lax.axis_index("grp"), lax.axis_index("col")
    others = [lax.rem(g + p, grp) for p in range(1, grp)]
    return g, [(other, (other, c)) for other in others]


def grp_stages(size):
    g, c = me_of(size)
    return [((g // (1 << t)) % 2, (flip(g, 1 << t), c)) for t in range(bits_of(size))]


def targets_of(groups):
    return [target for _, targets in groups for _, target in targets]


def square(x):
    high = x.astype(jnp.bfloat16)
    low = (x - high.astype(jnp.float32)).astype(jnp.bfloat16)

    def dot(p, q):
        return lax.dot_general(
            p, q, (((0,), (0,)), ((), ())), preferred_element_type=jnp.float32
        )

    cross = dot(high, low)
    return dot(high, high) + (cross + cross.T)


def gram_blocks(rank, grams, devices):
    side = rank // LANES
    upper = [(w, r, c) for w in range(grams) for r in range(side) for c in range(r, side)]
    if len(upper) * LANES % (8 * devices) == 0:
        return upper
    return [(w, r, c) for w in range(grams) for r in range(side) for c in range(side)]


def pack_gram(blocks, which, gram, ref):
    for number, (w, r, c) in enumerate(blocks):
        if w == which:
            ref[number * LANES : (number + 1) * LANES, :] = gram[
                r * LANES : (r + 1) * LANES, c * LANES : (c + 1) * LANES
            ]


def unpack_gram(blocks, which, ref):
    found = {}
    for number, (w, r, c) in enumerate(blocks):
        if w == which:
            found[r, c] = ref[number * LANES : (number + 1) * LANES, :]
    for r, c in list(found):
        if (c, r) not in found:
            found[c, r] = found[r, c].T
    side = max(r for r, _ in found) + 1
    return jnp.concatenate(
        [jnp.concatenate([found[r, c] for c in range(side)], axis=1) for r in range(side)], axis=0
    )


def gather_kernel(
    grp, col, b_ref, c_ref, n_ref, b_out, c_out, product_out, third_out, n_out,
    acc, landing, full, *sems,
):
    g, c = me_of(grp)
    rank = b_ref.shape[1]
    groups = [core_group(), chip_group(col), grp_group(grp)]
    others = targets_of(groups[2:])
    greet(targets_of(groups))
    pending = [send(n_ref, n_out, sems[4:], 0, groups[0][1][0][1])]
    for which, (src, out) in enumerate(((c_ref, c_out), (b_ref, b_out))):
        size = src.shape[0]
        mine = out.at[rows_at(g * size, size), :]
        mine[...] = src[...].astype(jnp.bfloat16)
        for number, target in enumerate(others):
            pending.append(send(mine, mine, sems[2:], which * (grp - 1) + number, target))
    layout = gram_blocks(rank, 2, grp * col)
    pack_gram(layout, 0, square(b_ref[...]), acc)
    pack_gram(layout, 1, square(c_ref[...]), acc)
    offset, rows = scatter_all(groups, acc, landing, sems)
    full[rows_at(offset, rows), :] = acc[rows_at(offset, rows), :]
    spread_all(groups, full, sems, offset, rows)
    third = unpack_gram(layout, 1, full)
    product_out[...] = unpack_gram(layout, 0, full) * third
    third_out[...] = third
    for copy in pending:
        copy.wait()


def first_factor_kernel(
    grp, col, part_ref, inverse_ref, third_ref, update_out, low_out, two_out,
    acc, landing, full, gram, piece, whole, other_inverse, *sems,
):
    g, c = me_of(grp)
    total, gram_rank = part_ref.shape
    own = total // col
    groups = [core_group(), chip_group(col)]
    others = targets_of([grp_group(grp)])
    greet(others + targets_of(groups))
    given = send(inverse_ref, other_inverse, sems[4:], 0, groups[0][1][0][1])
    for block in range(col):
        spot = (block % 2 * (col // 2) + block // 2) * own
        acc[spot : spot + own, :] = part_ref[block * own : (block + 1) * own, :]
    offset, rows = scatter_all(groups, acc, landing, sems)
    given.wait()
    update = jnp.dot(
        acc[rows_at(offset, rows), :],
        inverse_ref[...] + other_inverse[...],
        precision=HIGHEST,
        preferred_element_type=jnp.float32,
    )
    update_out[...] = update
    full[rows_at(offset, rows), :] = update
    spread_all(groups, full, sems, offset, rows)
    layout = gram_blocks(gram_rank, 1, grp)
    pack_gram(layout, 0, square(full[...]), gram)
    groups = [grp_group(grp)]
    offset, rows = scatter_all(groups, gram, piece, sems[2:])
    whole[rows_at(offset, rows), :] = gram[rows_at(offset, rows), :]
    spread_all(groups, whole, sems[2:], offset, rows)
    gram_first = unpack_gram(layout, 0, whole)
    row = lax.broadcasted_iota(jnp.int32, gram_first.shape, 0)
    column = lax.broadcasted_iota(jnp.int32, gram_first.shape, 1)
    diagonal = jnp.where(row == column, gram_first, 0.0)
    norm_row = jnp.sqrt(jnp.sum(diagonal, axis=0, keepdims=True) + 1e-06)
    norm_col = jnp.sqrt(jnp.sum(diagonal, axis=1, keepdims=True) + 1e-06)
    two_out[...] = gram_first / (norm_col * norm_row) * third_ref[...]
    for block in range(col):
        first = (block % 2 * (col // 2) + block // 2) * own
        low_out[block * own : (block + 1) * own, :] = (
            full[first : first + own, :] / norm_row
        ).astype(jnp.bfloat16)


def second_factor_kernel(grp, part_ref, gram_ref, out_ref, warm_out, landing, *sems):
    g, c = me_of(grp)
    count = bits_of(grp)
    own = part_ref.shape[0] // grp
    greet([target for _, target in grp_stages(grp)])
    half = part_ref.shape[1] // 2
    holding = []
    for h in range(2):
        lanes = slice(h * half, (h + 1) * half)
        holding.append(
            {m: part_ref.at[rows_at(flip(g, m) * own, own), lanes] for m in range(grp)}
        )
    spare = [0, 0]
    used = 0
    for stage in range(count):
        copies = []
        for h in range(2):
            bit = stage if h == 0 else count - 1 - stage
            target = (flip(g, 1 << bit), c)
            for m in sorted(holding[h]):
                if not (m >> bit) & 1:
                    place = landing.at[h, spare[h]]
                    spare[h] += 1
                    source = holding[h][m | (1 << bit)]
                    copies.append((h, m, bit, place, send(source, place, sems, used, target)))
                    used += 1
        if stage == 0:
            eye, unit, _, _, x, r = scaled_gram(gram_ref[...])
            unit_low = unit.astype(jnp.bfloat16)
            warm_out[...], _ = lax.fori_loop(
                0, WARM_STEPS, lambda _, state: low_step(eye, unit_low, *state), (x, r)
            )
        for h, m, bit, place, copy in copies:
            copy.wait()
            place[...] += holding[h][m][...]
            holding[h][m] = place
            del holding[h][m | (1 << bit)]
    for h in range(2):
        out_ref[:, h * half : (h + 1) * half] = holding[h][0][...]


def remote_call(kernel, number, args, outs, scratch):
    vmem = pl.BlockSpec(memory_space=pltpu.VMEM)
    return pl.pallas_call(
        kernel,
        out_shape=[jax.ShapeDtypeStruct(shape, dtype) for shape, dtype in outs],
        in_specs=[vmem] * len(args),
        out_specs=[vmem] * len(outs),
        scratch_shapes=scratch,
        compiler_params=pltpu.CompilerParams(
            collective_id=number, has_side_effects=True, vmem_limit_bytes=VMEM_LIMIT
        ),
    )(*args)


def semaphores(count):
    return [pltpu.SemaphoreType.DMA((count,))] * 2


def on_device(blocks, i_index, j_index, k_index, block_count, b_factor, c_factor):
    edge = blocks.shape[1]
    rank = b_factor.shape[1]
    grp, col = lax.axis_size("grp"), lax.axis_size("col")
    col_links = col // 2
    f32, bf16 = jnp.float32, jnp.bfloat16
    gram_rows = len(gram_blocks(rank, 2, grp * col)) * LANES
    first_gram = len(gram_blocks(rank, 1, grp)) * LANES
    b_range, c_range, gram_one, gram_third, twin_count = remote_call(
        functools.partial(gather_kernel, grp, col),
        0,
        (b_factor, c_factor, jnp.broadcast_to(block_count.astype(f32), (8, LANES))),
        [
            ((grp * b_factor.shape[0], rank), bf16),
            ((grp * c_factor.shape[0], rank), bf16),
            ((rank, rank), f32),
            ((rank, rank), f32),
            ((8, LANES), f32),
        ],
        [
            pltpu.VMEM((gram_rows, LANES), f32),
            pltpu.VMEM((gram_rows, LANES), f32),
            pltpu.VMEM((gram_rows, LANES), f32),
        ]
        + semaphores(2 * (col_links + grp - 1))
        + semaphores(2 * (grp - 1))
        + semaphores(1),
    )
    twin = twin_count[0, :1].astype(jnp.int32)
    core = lax.axis_index("col") % 2
    lead = jnp.where(block_count == twin, core == 0, block_count < twin).astype(jnp.int32)
    scalars = (i_index, j_index, k_index, block_count)
    own_rows = 2 * edge
    first_rows = own_rows * col
    partial_one = mode_call(mode_one_kernel, scalars, blocks, b_range, c_range, first_rows, [])
    a_update, a_range, gram_two = remote_call(
        functools.partial(first_factor_kernel, grp, col),
        1,
        (partial_one, inverse(lead, gram_one), gram_third),
        [((own_rows, rank), f32), ((first_rows, rank), bf16), ((rank, rank), f32)],
        [
            pltpu.VMEM((first_rows, rank), f32),
            pltpu.VMEM((first_rows, rank), f32),
            pltpu.VMEM((first_rows, rank), f32),
            pltpu.VMEM((first_gram, LANES), f32),
            pltpu.VMEM((first_gram, LANES), f32),
            pltpu.VMEM((first_gram, LANES), f32),
            pltpu.VMEM((rank, rank), f32),
        ]
        + semaphores(2 * col_links)
        + semaphores(2 * (grp - 1))
        + semaphores(1),
    )
    second_rows = b_range.shape[0]
    partial_two = mode_call(
        mode_two_kernel,
        scalars,
        blocks,
        a_range,
        c_range,
        second_rows,
        [pltpu.VMEM((UNROLL, 8 * edge, LANES), f32)],
    )
    own_sum, warm = remote_call(
        functools.partial(second_factor_kernel, grp),
        2,
        (partial_two, gram_two),
        [((second_rows // grp, rank), f32), ((rank, rank), f32)],
        [pltpu.VMEM((2, grp - 1, second_rows // grp, rank // 2), f32)]
        + semaphores(2 * (grp - 1)),
    )
    b_update = pl.pallas_call(
        solve_kernel,
        out_shape=jax.ShapeDtypeStruct(own_sum.shape, f32),
        in_specs=[pl.BlockSpec(memory_space=pltpu.VMEM)] * 3,
        out_specs=pl.BlockSpec(memory_space=pltpu.VMEM),
        compiler_params=pltpu.CompilerParams(vmem_limit_bytes=VMEM_LIMIT),
    )(own_sum, gram_two, warm)
    return (a_update, b_update)


def solution(mesh):
    return jax.shard_map(
        on_device,
        mesh=mesh,
        in_specs=(
            P(("grp", "col"), None, None),
            P(("grp", "col")),
            P(("grp", "col")),
            P(("grp", "col")),
            P(("grp", "col")),
            P(("grp", "col"), None),
            P(("grp", "col"), None),
        ),
        out_specs=(P(("grp", "col"), None), P(("grp", "col"), None)),
        check_vma=False,
    )
```

```python
import functools
import jax
import jax.numpy as jnp
from jax import lax
from jax.experimental import pallas as pl
from jax.experimental.pallas import tpu as pltpu
from jax.sharding import PartitionSpec as P

HIGHEST = lax.Precision.HIGHEST
GROUP = 32
UNROLL = 32
WARM_STEPS = 10
QUARTER = 32
LANES = 128
VMEM_LIMIT = 56 * 1024 * 1024


def khatri_rao(left, tail, first):
    rows = [
        jnp.broadcast_to(left[first + t : first + t + 1, :], tail.shape).astype(jnp.bfloat16) * tail
        for t in range(8)
    ]
    return jnp.concatenate(rows, axis=0)


def product_rows(lhs_part, left, tail):
    total = None
    for q in range(4):
        term = jnp.dot(
            lhs_part(q), khatri_rao(left, tail, 8 * q), preferred_element_type=jnp.float32
        )
        total = term if total is None else total + term
    return total


def slot_loop(count, do_slot):
    base = pl.program_id(0) * GROUP
    steps = jnp.clip((count - base + UNROLL - 1) // UNROLL, 0, GROUP // UNROLL)

    def body(step, carry):
        for u in range(UNROLL):
            local = step * UNROLL + u
            do_slot(local, base + local, u)
        return carry

    lax.fori_loop(0, steps, body, 0)


def mode_one_kernel(i_ref, j_ref, k_ref, n_ref, x_ref, b_ref, c_ref, out_ref):
    @pl.when(pl.program_id(0) == 0)
    def _():
        out_ref[...] = jnp.zeros_like(out_ref)

    count = n_ref[0]

    def do_slot(local, slot, u):
        left = b_ref[pl.ds(pl.multiple_of(j_ref[slot] * 32, 32), 32), :].astype(jnp.float32)
        tail = c_ref[pl.ds(pl.multiple_of(k_ref[slot] * 32, 32), 32), :]
        result = product_rows(lambda q: x_ref[local, :, q * 256 : (q + 1) * 256], left, tail)
        alive = (slot < count).astype(jnp.float32)
        rows = pl.ds(pl.multiple_of(i_ref[slot] * 32, 32), 32)
        out_ref[rows, :] += result * alive

    slot_loop(count, do_slot)


def quarter_swap(parts):
    lane = lax.broadcasted_iota(jnp.int32, parts[0].shape, 1)
    even = (lane // QUARTER) % 2 == 0
    low = lane < 2 * QUARTER

    def pair(p, q, keep, dist):
        return (
            jnp.where(keep, p, pltpu.roll(q, dist, 1)),
            jnp.where(keep, pltpu.roll(p, LANES - dist, 1), q),
        )

    p0, p1 = pair(parts[0], parts[1], even, QUARTER)
    p2, p3 = pair(parts[2], parts[3], even, QUARTER)
    r0, r2 = pair(p0, p2, low, 2 * QUARTER)
    r1, r3 = pair(p1, p3, low, 2 * QUARTER)
    return [r0, r1, r2, r3]


def mode_two_kernel(i_ref, j_ref, k_ref, n_ref, x_ref, a_ref, c_ref, out_ref, wide):
    @pl.when(pl.program_id(0) == 0)
    def _():
        out_ref[...] = jnp.zeros_like(out_ref)

    count = n_ref[0]

    def do_slot(local, slot, u):
        for col in range(8):
            wide[u, 32 * col : 32 * col + 32, :] = x_ref[
                local, :, col * LANES : (col + 1) * LANES
            ].astype(jnp.float32)

        def lhs_part(q):
            pieces = []
            for half in range(2):
                first = q * 8 + half * 4
                parts = [wide[u, pl.ds(first + t, 8, stride=32), :] for t in range(4)]
                pieces.append(jnp.concatenate(quarter_swap(parts), axis=0).astype(jnp.bfloat16))
            return jnp.concatenate(pieces, axis=1)

        left = a_ref[pl.ds(pl.multiple_of(i_ref[slot] * 32, 32), 32), :].astype(jnp.float32)
        tail = c_ref[pl.ds(pl.multiple_of(k_ref[slot] * 32, 32), 32), :]
        result = product_rows(lhs_part, left, tail)
        alive = (slot < count).astype(jnp.float32)
        rows = pl.ds(pl.multiple_of(j_ref[slot] * 32, 32), 32)
        out_ref[rows, :] += result * alive

    slot_loop(count, do_slot)


def mode_call(kernel, scalars, blocks, left, tail, rows, scratch):
    slots, edge, width = blocks.shape
    rank = left.shape[1]
    grid_spec = pltpu.PrefetchScalarGridSpec(
        num_scalar_prefetch=4,
        grid=(slots // GROUP,),
        in_specs=[
            pl.BlockSpec((GROUP, edge, width), lambda g, *_: (g, 0, 0)),
            pl.BlockSpec(left.shape, lambda g, *_: (0, 0)),
            pl.BlockSpec(tail.shape, lambda g, *_: (0, 0)),
        ],
        out_specs=pl.BlockSpec((rows, rank), lambda g, *_: (0, 0)),
        scratch_shapes=scratch,
    )
    return pl.pallas_call(
        kernel,
        grid_spec=grid_spec,
        out_shape=jax.ShapeDtypeStruct((rows, rank), jnp.float32),
        compiler_params=pltpu.CompilerParams(vmem_limit_bytes=VMEM_LIMIT),
        cost_estimate=pl.CostEstimate(
            flops=2 * slots * edge * width * rank,
            bytes_accessed=2 * slots * edge * width,
            transcendentals=0,
        ),
    )(*scalars, blocks, left, tail)


def inverse_kernel(mine_ref, twin_ref, g_ref, out_ref):
    lead = jnp.max(mine_ref[...]) < jnp.max(twin_ref[...])

    @pl.when(jnp.logical_not(lead))
    def _():
        out_ref[...] = jnp.zeros_like(out_ref)

    @pl.when(lead)
    def _():
        out_ref[...] = newton_inverse(g_ref[...])


def scaled_gram(gram):
    row = lax.broadcasted_iota(jnp.int32, gram.shape, 0)
    col = lax.broadcasted_iota(jnp.int32, gram.shape, 1)
    eye = (row == col).astype(jnp.float32)
    scale_row = lax.rsqrt(jnp.sum(gram * eye, axis=0, keepdims=True))
    scale_col = lax.rsqrt(jnp.sum(gram * eye, axis=1, keepdims=True))
    unit = gram * scale_row * scale_col
    bound = 1.0 / jnp.max(jnp.sum(jnp.abs(unit), axis=0, keepdims=True))
    return eye, unit, scale_row, scale_col, eye * bound, eye - unit * bound


def low_step(eye, unit_low, x, r):
    x = x + jnp.dot(
        x.astype(jnp.bfloat16), r.astype(jnp.bfloat16), preferred_element_type=jnp.float32
    )
    r = eye - jnp.dot(unit_low, x.astype(jnp.bfloat16), preferred_element_type=jnp.float32)
    return x, r


def finish_inverse(scaled, x):
    eye, unit, scale_row, scale_col, start, start_r = scaled

    def residual(x):
        return eye - jnp.dot(unit, x, precision=HIGHEST, preferred_element_type=jnp.float32)

    def update(x, r):
        return x + jnp.dot(x, r, precision=HIGHEST, preferred_element_type=jnp.float32)

    def body(state):
        step, _, x, r = state
        x = update(x, r)
        r = residual(x)
        return step + 1, jnp.sum(r * r), x, r

    def more(state):
        return jnp.logical_and(state[0] < 60, state[1] > 1e-6)

    r = residual(x)
    good = jnp.sum(r * r) < 0.25
    x = jnp.where(good, x, start)
    r = jnp.where(good, r, start_r)
    _, _, x, r = lax.while_loop(more, body, (jnp.int32(0), jnp.sum(r * r), x, r))
    return update(x, r) * scale_row * scale_col


def newton_inverse(gram):
    scaled = scaled_gram(gram)
    eye, unit, _, _, start, start_r = scaled
    unit_low = unit.astype(jnp.bfloat16)

    def body_low(state):
        step, _, x, r = state
        x, r = low_step(eye, unit_low, x, r)
        return step + 1, jnp.sum(r * r), x, r

    def more_low(state):
        return jnp.logical_and(state[0] < 16, state[1] > 0.01)

    _, _, x, _ = lax.while_loop(
        more_low, body_low, (jnp.int32(0), jnp.sum(start_r * start_r), start, start_r)
    )
    return finish_inverse(scaled, x)


def inverse(mine, twin, gram):
    return pl.pallas_call(
        inverse_kernel,
        out_shape=jax.ShapeDtypeStruct(gram.shape, jnp.float32),
        in_specs=[pl.BlockSpec(memory_space=pltpu.VMEM)] * 3,
        out_specs=pl.BlockSpec(memory_space=pltpu.VMEM),
        compiler_params=pltpu.CompilerParams(vmem_limit_bytes=VMEM_LIMIT),
    )(mine, twin, gram)


def solve_kernel(sum_ref, gram_ref, warm_ref, out_ref):
    own, rank = sum_ref.shape
    solved = jnp.dot(
        sum_ref[...],
        finish_inverse(scaled_gram(gram_ref[...]), warm_ref[...]),
        precision=HIGHEST,
        preferred_element_type=jnp.float32,
    )
    out_ref[...] = solved.reshape(own // 32, 4, 8, rank).swapaxes(1, 2).reshape(own, rank)


def me_of(shape):
    return lax.axis_index("grp"), lax.axis_index("col")


def bits_of(size):
    count = size.bit_length() - 1
    assert size == 1 << count
    return count


def flip(position, mask):
    out = position
    for t in range(mask.bit_length()):
        if (mask >> t) & 1:
            bit = (position // (1 << t)) % 2
            out = out + (1 - 2 * bit) * (1 << t)
    return out


def greet(targets):
    barrier = pltpu.get_barrier_semaphore()
    for target in targets:
        pl.semaphore_signal(barrier, inc=1, device_id=target, device_id_type=pl.DeviceIdType.MESH)
    pl.semaphore_wait(barrier, len(targets))


def send(src, dst, sems, index, target):
    copy = pltpu.make_async_remote_copy(
        src_ref=src,
        dst_ref=dst,
        send_sem=sems[0].at[index],
        recv_sem=sems[1].at[index],
        device_id=target,
        device_id_type=pl.DeviceIdType.MESH,
    )
    copy.start()
    return copy


def rows_at(first, size):
    return pl.ds(pl.multiple_of(first, 8), size)


def scatter_sum(group, acc, landing, sems, first, offset, rows):
    index, targets = group
    size = len(targets) + 1
    chunk = rows // size
    copies = []
    for number, (other, target) in enumerate(targets):
        place = landing.at[pl.ds(rows - (number + 1) * chunk, chunk), :]
        copies.append(
            send(acc.at[rows_at(offset + other * chunk, chunk), :], place, sems, first + number, target)
        )
    offset = offset + index * chunk
    for number, copy in enumerate(copies):
        copy.wait()
        low = rows - (number + 1) * chunk
        acc[rows_at(offset, chunk), :] += landing[low : low + chunk, :]
    return offset, chunk


def spread(group, full, sems, first, offset, rows):
    index, targets = group
    copies = []
    mine = full.at[rows_at(offset, rows), :]
    for number, (_, target) in enumerate(targets):
        copies.append(send(mine, mine, sems, first + number, target))
    for copy in copies:
        copy.wait()
    return offset - index * rows, rows * (len(targets) + 1)


def scatter_all(groups, acc, landing, sems):
    offset, rows, first = jnp.int32(0), acc.shape[0], 0
    for group in groups:
        offset, rows = scatter_sum(group, acc, landing, sems, first, offset, rows)
        first += len(group[1])
    return offset, rows


def spread_all(groups, full, sems, offset, rows):
    first = sum(len(group[1]) for group in groups)
    for group in reversed(groups):
        offset, rows = spread(group, full, sems, first, offset, rows)
        first += len(group[1])


def core_group():
    g, c = lax.axis_index("grp"), lax.axis_index("col")
    core = lax.rem(c, 2)
    return core, [(1 - core, (g, c + 1 - 2 * core))]


def chip_group(col):
    g, c = lax.axis_index("grp"), lax.axis_index("col")
    chips, core, chip = col // 2, lax.rem(c, 2), c // 2
    others = [lax.rem(chip + p, chips) for p in range(1, chips)]
    return chip, [(other, (g, other * 2 + core)) for other in others]


def grp_group(grp):
    g, c = lax.axis_index("grp"), lax.axis_index("col")
    others = [lax.rem(g + p, grp) for p in range(1, grp)]
    return g, [(other, (other, c)) for other in others]


def grp_stages(size):
    g, c = me_of(size)
    return [((g // (1 << t)) % 2, (flip(g, 1 << t), c)) for t in range(bits_of(size))]


def targets_of(groups):
    return [target for _, targets in groups for _, target in targets]


def square(x):
    high = x.astype(jnp.bfloat16)
    low = (x - high.astype(jnp.float32)).astype(jnp.bfloat16)

    def dot(p, q):
        return lax.dot_general(
            p, q, (((0,), (0,)), ((), ())), preferred_element_type=jnp.float32
        )

    cross = dot(high, low)
    return dot(high, high) + (cross + cross.T)


def gram_blocks(rank, grams, devices):
    side = rank // LANES
    upper = [(w, r, c) for w in range(grams) for r in range(side) for c in range(r, side)]
    if len(upper) * LANES % (8 * devices) == 0:
        return upper
    return [(w, r, c) for w in range(grams) for r in range(side) for c in range(side)]


def pack_gram(blocks, which, gram, ref):
    for number, (w, r, c) in enumerate(blocks):
        if w == which:
            ref[number * LANES : (number + 1) * LANES, :] = gram[
                r * LANES : (r + 1) * LANES, c * LANES : (c + 1) * LANES
            ]


def unpack_gram(blocks, which, ref):
    found = {}
    for number, (w, r, c) in enumerate(blocks):
        if w == which:
            found[r, c] = ref[number * LANES : (number + 1) * LANES, :]
    for r, c in list(found):
        if (c, r) not in found:
            found[c, r] = found[r, c].T
    side = max(r for r, _ in found) + 1
    return jnp.concatenate(
        [jnp.concatenate([found[r, c] for c in range(side)], axis=1) for r in range(side)], axis=0
    )


def gather_kernel(
    grp, col, b_ref, c_ref, n_ref, b_out, c_out, product_out, third_out, n_out,
    acc, landing, full, *sems,
):
    g, c = me_of(grp)
    rank = b_ref.shape[1]
    groups = [core_group(), chip_group(col), grp_group(grp)]
    others = targets_of(groups[2:])
    greet(targets_of(groups))
    pending = [send(n_ref, n_out, sems[4:], 0, groups[0][1][0][1])]
    for which, (src, out) in enumerate(((c_ref, c_out), (b_ref, b_out))):
        size = src.shape[0]
        mine = out.at[rows_at(g * size, size), :]
        mine[...] = src[...].astype(jnp.bfloat16)
        for number, target in enumerate(others):
            pending.append(send(mine, mine, sems[2:], which * (grp - 1) + number, target))
    layout = gram_blocks(rank, 2, grp * col)
    pack_gram(layout, 0, square(b_ref[...]), acc)
    pack_gram(layout, 1, square(c_ref[...]), acc)
    offset, rows = scatter_all(groups, acc, landing, sems)
    full[rows_at(offset, rows), :] = acc[rows_at(offset, rows), :]
    spread_all(groups, full, sems, offset, rows)
    third = unpack_gram(layout, 1, full)
    product_out[...] = unpack_gram(layout, 0, full) * third
    third_out[...] = third
    for copy in pending:
        copy.wait()


def first_factor_kernel(
    grp, col, part_ref, inverse_ref, third_ref, update_out, low_out, two_out,
    acc, landing, full, gram, piece, whole, other_inverse, *sems,
):
    g, c = me_of(grp)
    total, gram_rank = part_ref.shape
    own = total // col
    groups = [core_group(), chip_group(col)]
    others = targets_of([grp_group(grp)])
    greet(others + targets_of(groups))
    given = send(inverse_ref, other_inverse, sems[4:], 0, groups[0][1][0][1])
    for block in range(col):
        spot = (block % 2 * (col // 2) + block // 2) * own
        acc[spot : spot + own, :] = part_ref[block * own : (block + 1) * own, :]
    offset, rows = scatter_all(groups, acc, landing, sems)
    given.wait()
    update = jnp.dot(
        acc[rows_at(offset, rows), :],
        inverse_ref[...] + other_inverse[...],
        precision=HIGHEST,
        preferred_element_type=jnp.float32,
    )
    update_out[...] = update
    full[rows_at(offset, rows), :] = update
    spread_all(groups, full, sems, offset, rows)
    layout = gram_blocks(gram_rank, 1, grp)
    pack_gram(layout, 0, square(full[...]), gram)
    groups = [grp_group(grp)]
    offset, rows = scatter_all(groups, gram, piece, sems[2:])
    whole[rows_at(offset, rows), :] = gram[rows_at(offset, rows), :]
    spread_all(groups, whole, sems[2:], offset, rows)
    gram_first = unpack_gram(layout, 0, whole)
    row = lax.broadcasted_iota(jnp.int32, gram_first.shape, 0)
    column = lax.broadcasted_iota(jnp.int32, gram_first.shape, 1)
    diagonal = jnp.where(row == column, gram_first, 0.0)
    norm_row = jnp.sqrt(jnp.sum(diagonal, axis=0, keepdims=True) + 1e-06)
    norm_col = jnp.sqrt(jnp.sum(diagonal, axis=1, keepdims=True) + 1e-06)
    two_out[...] = gram_first / (norm_col * norm_row) * third_ref[...]
    for block in range(col):
        first = (block % 2 * (col // 2) + block // 2) * own
        low_out[block * own : (block + 1) * own, :] = (
            full[first : first + own, :] / norm_row
        ).astype(jnp.bfloat16)


def second_factor_kernel(grp, part_ref, gram_ref, out_ref, warm_out, landing, *sems):
    g, c = me_of(grp)
    count = bits_of(grp)
    own = part_ref.shape[0] // grp
    greet([target for _, target in grp_stages(grp)])
    half = part_ref.shape[1] // 2
    holding = []
    for h in range(2):
        lanes = slice(h * half, (h + 1) * half)
        holding.append(
            {m: part_ref.at[rows_at(flip(g, m) * own, own), lanes] for m in range(grp)}
        )
    spare = [0, 0]
    used = 0
    for stage in range(count):
        copies = []
        for h in range(2):
            bit = stage if h == 0 else count - 1 - stage
            target = (flip(g, 1 << bit), c)
            for m in sorted(holding[h]):
                if not (m >> bit) & 1:
                    place = landing.at[h, spare[h]]
                    spare[h] += 1
                    source = holding[h][m | (1 << bit)]
                    copies.append((h, m, bit, place, send(source, place, sems, used, target)))
                    used += 1
        if stage == 0:
            eye, unit, _, _, x, r = scaled_gram(gram_ref[...])
            unit_low = unit.astype(jnp.bfloat16)
            warm_out[...], _ = lax.fori_loop(
                0, WARM_STEPS, lambda _, state: low_step(eye, unit_low, *state), (x, r)
            )
        for h, m, bit, place, copy in copies:
            copy.wait()
            place[...] += holding[h][m][...]
            holding[h][m] = place
            del holding[h][m | (1 << bit)]
    for h in range(2):
        out_ref[:, h * half : (h + 1) * half] = holding[h][0][...]


def remote_call(kernel, number, args, outs, scratch):
    vmem = pl.BlockSpec(memory_space=pltpu.VMEM)
    return pl.pallas_call(
        kernel,
        out_shape=[jax.ShapeDtypeStruct(shape, dtype) for shape, dtype in outs],
        in_specs=[vmem] * len(args),
        out_specs=[vmem] * len(outs),
        scratch_shapes=scratch,
        compiler_params=pltpu.CompilerParams(
            collective_id=number, has_side_effects=True, vmem_limit_bytes=VMEM_LIMIT
        ),
    )(*args)


def semaphores(count):
    return [pltpu.SemaphoreType.DMA((count,))] * 2


def on_device(blocks, i_index, j_index, k_index, block_count, b_factor, c_factor):
    edge = blocks.shape[1]
    rank = b_factor.shape[1]
    grp, col = lax.axis_size("grp"), lax.axis_size("col")
    col_links = col // 2
    f32, bf16 = jnp.float32, jnp.bfloat16
    gram_rows = len(gram_blocks(rank, 2, grp * col)) * LANES
    first_gram = len(gram_blocks(rank, 1, grp)) * LANES
    load = 2 * block_count + lax.axis_index("col") % 2
    load_key = jnp.broadcast_to(load.astype(f32), (8, LANES))
    b_range, c_range, gram_one, gram_third, twin_key = remote_call(
        functools.partial(gather_kernel, grp, col),
        0,
        (b_factor, c_factor, load_key),
        [
            ((grp * b_factor.shape[0], rank), bf16),
            ((grp * c_factor.shape[0], rank), bf16),
            ((rank, rank), f32),
            ((rank, rank), f32),
            ((8, LANES), f32),
        ],
        [
            pltpu.VMEM((gram_rows, LANES), f32),
            pltpu.VMEM((gram_rows, LANES), f32),
            pltpu.VMEM((gram_rows, LANES), f32),
        ]
        + semaphores(2 * (col_links + grp - 1))
        + semaphores(2 * (grp - 1))
        + semaphores(1),
    )
    scalars = (i_index, j_index, k_index, block_count)
    own_rows = 2 * edge
    first_rows = own_rows * col
    partial_one = mode_call(mode_one_kernel, scalars, blocks, b_range, c_range, first_rows, [])
    a_update, a_range, gram_two = remote_call(
        functools.partial(first_factor_kernel, grp, col),
        1,
        (partial_one, inverse(load_key, twin_key, gram_one), gram_third),
        [((own_rows, rank), f32), ((first_rows, rank), bf16), ((rank, rank), f32)],
        [
            pltpu.VMEM((first_rows, rank), f32),
            pltpu.VMEM((first_rows, rank), f32),
            pltpu.VMEM((first_rows, rank), f32),
            pltpu.VMEM((first_gram, LANES), f32),
            pltpu.VMEM((first_gram, LANES), f32),
            pltpu.VMEM((first_gram, LANES), f32),
            pltpu.VMEM((rank, rank), f32),
        ]
        + semaphores(2 * col_links)
        + semaphores(2 * (grp - 1))
        + semaphores(1),
    )
    second_rows = b_range.shape[0]
    partial_two = mode_call(
        mode_two_kernel,
        scalars,
        blocks,
        a_range,
        c_range,
        second_rows,
        [pltpu.VMEM((UNROLL, 8 * edge, LANES), f32)],
    )
    own_sum, warm = remote_call(
        functools.partial(second_factor_kernel, grp),
        2,
        (partial_two, gram_two),
        [((second_rows // grp, rank), f32), ((rank, rank), f32)],
        [pltpu.VMEM((2, grp - 1, second_rows // grp, rank // 2), f32)]
        + semaphores(2 * (grp - 1)),
    )
    b_update = pl.pallas_call(
        solve_kernel,
        out_shape=jax.ShapeDtypeStruct(own_sum.shape, f32),
        in_specs=[pl.BlockSpec(memory_space=pltpu.VMEM)] * 3,
        out_specs=pl.BlockSpec(memory_space=pltpu.VMEM),
        compiler_params=pltpu.CompilerParams(vmem_limit_bytes=VMEM_LIMIT),
    )(own_sum, gram_two, warm)
    return (a_update, b_update)


def solution(mesh):
    return jax.shard_map(
        on_device,
        mesh=mesh,
        in_specs=(
            P(("grp", "col"), None, None),
            P(("grp", "col")),
            P(("grp", "col")),
            P(("grp", "col")),
            P(("grp", "col")),
            P(("grp", "col"), None),
            P(("grp", "col"), None),
        ),
        out_specs=(P(("grp", "col"), None), P(("grp", "col"), None)),
        check_vma=False,
    )
```
